1024 devices in a mesh: rows: 256 (over x, z, core), cols: 4 (over y).
Axes of the slice: x: 4, y: 4, z: 32, core: 2. Of those that a mesh axis runs over, the one named last changes fastest.
Arguments:
- rhs: float32 [2048, 8192], P('rows', 'cols'), may hold values from -6 to 6
- cond_row: float32 [2048, 8192], P('rows', 'cols'), may hold values from 0.3 to 3
- cond_col: float32 [2048, 8192], P('rows', 'cols'), may hold values from 0.3 to 3
- leak: float32 [2048, 8192], P('rows', 'cols'), may hold values from 0.01 to 0.2
- agg_members: int32 [256, 4, 192, 128], P('rows', 'cols'), may hold values from -1 to 16383, as said below
- coarse_inverse: float32 [4, 1024, 1024], P('cols', 'rows'), as said below
Outputs:
- potential: float32 [2048, 8192], P('rows', 'cols')
The draws below stay inside these ranges and needn't reach their ends.
Inputs may be any that keep to these rules, and one draw needn't show every extreme that they name: `agg_members`: every node of a device's block is listed exactly once; aggregates are runs of consecutive node numbers in order, of 16 to 128 members, three consecutive aggregates covering 256 nodes, one of each three exactly 128; padding follows the members. Each coarse_inverse[c] is symmetric and positive definite.
All inputs are finite; a program needn't handle non-finite values.
Results may differ from the reference program's by a relative error of at most 0.0003.
Values sent between devices are 32-bit elements; how exact they have to be, the bound alone decides.
No kernel may reach another device: no remote copies, remote signals or barrier semaphores. Data moves between devices by JAX's collectives and lax.ppermute only.
A program may use at most 32 MiB of HBM per device.

```python
import math
import jax
import jax.numpy as jnp
from jax import lax

CX = 8
CY = 2048
COARSE_DEV = 4
NAGG = 192
COARSE = 1024
NX = 2048
NY = 8192
N_ROWS = 256
N_COLS = 4


def draw_agg_members(key, part):
    key = jax.random.fold_in(key, 5)
    first, second = jax.random.split(key)
    shape = (N_ROWS, N_COLS, NAGG // 3)
    middle = jax.random.randint(first, shape, 16, 113)
    rotate = jax.random.randint(second, shape, 0, 3)
    base = jnp.stack([jnp.full(shape, 128, jnp.int32), middle, 128 - middle], axis=-1)
    select = (jnp.arange(3, dtype=jnp.int32)[None, None, None, :] - rotate[..., None]) % 3
    sizes = jnp.take_along_axis(base, select, axis=-1).reshape(N_ROWS, N_COLS, NAGG)
    offsets = jnp.cumsum(sizes, axis=-1) - sizes
    slots = jnp.arange(128, dtype=jnp.int32)
    members = jnp.where(slots[None, None, None, :] < sizes[..., None], offsets[..., None] + slots[None, None, None, :], -1)
    return members.astype(jnp.int32)


def draw_coarse_inverse(key, part):
    key = jax.random.fold_in(key, 7)
    first, second = jax.random.split(key)
    noise = jax.random.normal(first, (N_COLS, COARSE, COARSE), jnp.float32)
    offdiag = (noise + jnp.swapaxes(noise, 1, 2)) * (0.35 / jnp.sqrt(2.0 * COARSE))
    diagonal = jax.random.uniform(second, (N_COLS, COARSE), jnp.float32, 1.0, 2.0)
    eye = jnp.eye(COARSE, dtype=jnp.float32)
    return 100.0 * (offdiag + eye[None, :, :] * diagonal[:, :, None])


def block_scale(own_key, dims, cuts, least, largest):
    def one(axis_at, blocks):
        steps = jax.random.uniform(jax.random.fold_in(jax.random.fold_in(own_key, 6), axis_at), (blocks,), jnp.float32, least / len(cuts), largest / len(cuts))
        return jnp.repeat(jnp.exp(steps), dims[axis_at] // blocks).reshape((-1,) + (1,) * (len(dims) - axis_at - 1))

    gain = one(*cuts[0])
    for cut in cuts[1:]:
        gain = gain * one(*cut)
    return gain


def bell_draw(rng, shape, scale, bound, cuts=(), kind=jnp.bfloat16):
    values = jax.random.normal(rng, shape, jnp.float32) * scale
    if len(cuts) > 0:
        values = block_scale(rng, shape, cuts, -0.22, 0.18) * values
    return jnp.clip(values, min=-bound, max=bound).astype(kind)


def setup_inputs(seed: int = 0) -> dict:
    streams_of = jax.random.split(jax.random.key(seed), 7)
    rhs = bell_draw(streams_of[0], (NX, NY), 1.0, 6.0, ((0, 256), (1, 4)), jnp.float32)
    cond_row = jnp.clip(jnp.exp(math.log(3.0) - 2.3025851 * jax.random.uniform(streams_of[1], (NX, NY), jnp.float32) ** block_scale(streams_of[1], (NX, NY), ((0, 256), (1, 4)), -0.2, 0.2)), 0.3, 3.0)
    cond_col = jnp.clip(jnp.exp(math.log(3.0) - 2.3025851 * jax.random.uniform(streams_of[2], (NX, NY), jnp.float32) ** block_scale(streams_of[2], (NX, NY), ((0, 256), (1, 4)), -0.2, 0.2)), 0.3, 3.0)
    leak = jnp.clip(jnp.exp(math.log(0.2) - 2.9957323 * jax.random.uniform(streams_of[3], (NX, NY), jnp.float32) ** block_scale(streams_of[3], (NX, NY), ((0, 256), (1, 4)), -0.2, 0.2)), 0.01, 0.2)
    agg_members = draw_agg_members(jax.random.fold_in(streams_of[6], 71), 0)
    coarse_inverse = draw_coarse_inverse(jax.random.fold_in(streams_of[6], 71), 0)
    return dict(rhs=rhs, cond_row=cond_row, cond_col=cond_col, leak=leak, agg_members=agg_members, coarse_inverse=coarse_inverse)


theta_cheb = 1.05
delta_cheb = 0.95
omega_sa = 2.0 / 3.0

def operate(field, cond_row, cond_col, west, north, diag):
    padded = jnp.pad(field, 1)
    out = diag * field - cond_row * padded[1:-1, 2:] - west * padded[1:-1, :-2]
    return out - cond_col * padded[2:, 1:-1] - north * padded[:-2, 1:-1]

def chebyshev(start, right, apply_op, diag):
    if start is None:
        resid = right
    else:
        resid = right - apply_op(start)
    step = resid / (theta_cheb * diag)
    value = step if start is None else start + step
    rho = delta_cheb / theta_cheb
    for turn in range(2):
        rho_new = 1.0 / (2.0 * theta_cheb / delta_cheb - rho)
        resid = resid - apply_op(step)
        step = rho_new * rho * step + 2.0 * rho_new / delta_cheb * (resid / diag)
        value = value + step
        rho = rho_new
    return value

def to_blocks(field):
    return field.reshape(N_ROWS, CX, N_COLS, CY).transpose(0, 2, 1, 3).reshape(N_ROWS, N_COLS, CX * CY)

def from_blocks(blocks):
    return blocks.reshape(N_ROWS, N_COLS, CX, CY).transpose(0, 2, 1, 3).reshape(N_ROWS * CX, N_COLS * CY)

def restrict_block(flat, members):
    valid = members >= 0
    index = jnp.where(valid, members, 0)
    counts = lax.optimization_barrier(jnp.sum(valid, axis=-1)).astype(jnp.float32)
    picked = jnp.where(valid, flat[index], jnp.float32(0.0))
    return lax.optimization_barrier(jnp.sum(picked, axis=-1)) / jnp.sqrt(counts)

def lift_block(values, members):
    valid = members >= 0
    index = jnp.where(valid, members, 0)
    counts = lax.optimization_barrier(jnp.sum(valid, axis=-1)).astype(jnp.float32)
    spread = jnp.where(valid, (values / jnp.sqrt(counts))[:, None], jnp.float32(0.0))
    return jnp.zeros((CX * CY,), jnp.float32).at[index.reshape(-1)].add(spread.reshape(-1))

def reference(rhs, cond_row, cond_col, leak, agg_members, coarse_inverse):
    west = jnp.pad(cond_row, ((0, 0), (1, 0)))[:, :-1]
    north = jnp.pad(cond_col, ((1, 0), (0, 0)))[:-1, :]
    diag = leak + cond_row + cond_col + west + north

    def apply_op(field):
        return operate(field, cond_row, cond_col, west, north, diag)
    pre = chebyshev(None, rhs, apply_op, diag)
    resid = rhs - apply_op(pre)
    smoothed = resid - omega_sa * apply_op(resid / diag)
    members = agg_members.reshape(N_ROWS * N_COLS, NAGG, 128)
    blocks = to_blocks(smoothed).reshape(N_ROWS * N_COLS, CX * CY)
    fine_coarse = jax.vmap(restrict_block)(blocks, members)
    group = NAGG // COARSE_DEV
    coarse_rhs = fine_coarse.reshape(N_ROWS, N_COLS, COARSE_DEV, group).sum(-1) / jnp.sqrt(jnp.float32(group))
    vectors = coarse_rhs.transpose(1, 0, 2).reshape(N_COLS, COARSE)
    coarse_corr = jnp.einsum('cij,cj->ci', coarse_inverse, vectors, precision=lax.Precision.HIGHEST)
    per_dev = coarse_corr.reshape(N_COLS, N_ROWS, COARSE_DEV).transpose(1, 0, 2)
    agg_vals = jnp.repeat(per_dev / jnp.sqrt(jnp.float32(group)), group, axis=-1).reshape(N_ROWS * N_COLS, NAGG)
    lifted_blocks = jax.vmap(lift_block)(agg_vals, members)
    lifted = from_blocks(lifted_blocks.reshape(N_ROWS, N_COLS, CX * CY))
    corrected = pre + lifted - omega_sa * apply_op(lifted) / diag
    return chebyshev(corrected, rhs, apply_op, diag)
```

```python
import functools

import jax
import jax.numpy as jnp
from jax import lax
from jax.experimental import pallas as pl
from jax.experimental.pallas import tpu as pltpu
from jax.sharding import Mesh
from jax.sharding import PartitionSpec as P

THETA = 1.05
DELTA = 0.95
OMEGA = 2.0 / 3.0
RHO0 = DELTA / THETA
RHO1 = 1.0 / (2.0 * THETA / DELTA - RHO0)
RHO2 = 1.0 / (2.0 * THETA / DELTA - RHO1)
LANES = 128
REACH = 5
WROWS = 24
MSG = 24
ROWAX = ("x", "z", "core")
VMEM_LIMIT = 48 * 1024 * 1024


def vmem():
    return pl.BlockSpec(memory_space=pltpu.VMEM)


def call(kernel, outs, nin, name):
    return pl.pallas_call(
        kernel,
        out_shape=outs,
        in_specs=[vmem()] * nin,
        out_specs=jax.tree.map(lambda _: vmem(), outs),
        compiler_params=pltpu.CompilerParams(vmem_limit_bytes=VMEM_LIMIT),
        name=name,
    )


def f32(*shape):
    return jax.ShapeDtypeStruct(shape, jnp.float32)


def pack_rows(group, rhs, cr, cc, lk, agg, m, w_ref, mflat, up, down):
    width = rhs.shape[1]
    pairs = width // 256
    per_row = 3 * pairs
    lane = lax.broadcasted_iota(jnp.int32, (8, LANES), 1)
    row = lax.broadcasted_iota(jnp.int32, (8, LANES), 0)
    for j in range(pairs):
        base = (row * pairs + j) * 256
        p1 = agg[pl.ds(3 * j + 1, 8, stride=per_row), :]
        p2 = agg[pl.ds(3 * j + 2, 8, stride=per_row), :]
        p1 = jnp.broadcast_to(p1[:, 0:1], (8, LANES)) - base
        p2 = jnp.broadcast_to(p2[:, 0:1], (8, LANES)) - base
        s0 = 1.0 / jnp.sqrt(p1.astype(jnp.float32) * float(group))
        s1 = 1.0 / jnp.sqrt((p2 - p1).astype(jnp.float32) * float(group))
        s2 = 1.0 / jnp.sqrt((256 - p2).astype(jnp.float32) * float(group))
        for half in range(2):
            at = lane + half * LANES
            value = jnp.where(at < p1, s0, jnp.where(at < p2, s1, s2))
            w_ref[:, (2 * j + half) * LANES : (2 * j + half + 1) * LANES] = value
    tiles = m.shape[1] // LANES
    for k in range(m.shape[0]):
        for t in range(tiles):
            mflat[k * tiles + t : k * tiles + t + 1, :] = m[k : k + 1, t * LANES : (t + 1) * LANES]
    ncol = width // LANES
    keep = (row == 3).astype(jnp.float32)
    for t in range(ncol):
        s = slice(t * LANES, (t + 1) * LANES)
        a, b, c, d, e = rhs[:, s], lk[:, s], cr[:, s], cc[:, s], w_ref[:, s]
        up[MSG * t : MSG * (t + 1), :] = jnp.concatenate([a[0:5], b[0:5], c[0:5], d[0:5], e[0:4]], axis=0)
        north = keep * pltpu.roll(d, 1, 0)
        b = b + north
        down[MSG * t : MSG * (t + 1), :] = jnp.concatenate([a[3:8], b[3:8], c[3:8], d[3:8], e[4:8]], axis=0)
    half = 2 * tiles
    up[MSG * ncol : MSG * ncol + half, :] = mflat[0:half, :]
    down[MSG * ncol : MSG * ncol + half, :] = mflat[half : 2 * half, :]


def windows(own, above, below):
    zeros = jnp.zeros((3, LANES), jnp.float32)
    out = []
    for i in range(5):
        n = 4 if i == 4 else REACH
        at = 5 * i
        top, low = above[at : at + n], below[at : at + n]
        pad = jnp.zeros((8 - n, LANES), jnp.float32)
        out.append(jnp.concatenate([pad, top, own[i], low, pad], axis=0))
    return out


def pack_cols(rhs, cr, cc, lk, w, mflat, above, below, left, right):
    ncol = rhs.shape[1] // LANES
    half = mflat.shape[0] // 2
    for t, out in ((0, left), (ncol - 1, right)):
        s = slice(t * LANES, (t + 1) * LANES)
        own = [r[:, s] for r in (rhs, lk, cr, cc, w)]
        rows = slice(MSG * t, MSG * (t + 1))
        for i, value in enumerate(windows(own, above[rows, :], below[rows, :])):
            out[WROWS * i : WROWS * (i + 1), :] = value
        at = 5 * WROWS
        out[at : at + half, :] = above[MSG * ncol : MSG * ncol + half, :]
        out[at + half : at + 3 * half, :] = mflat[...]
        out[at + 3 * half : at + 4 * half, :] = below[MSG * ncol : MSG * ncol + half, :]


def shifted(v):
    n = v.shape[1]
    r = v.shape[0]
    return (pltpu.roll(v, n - 1, 1), pltpu.roll(v, 1, 1), pltpu.roll(v, r - 1, 0), pltpu.roll(v, 1, 0))


def scaled_apply(v, east, west, south, north):
    e, w, s, n = shifted(v)
    return v - east * e - west * w - south * s - north * n


def middle(zsize, rhs, cr, cc, lk, w, above, below, left, right, pre_o, z_o, w_o, east_o, west_o, south_o, north_o, msg):
    width = rhs.shape[1]
    ncol = width // LANES
    pieces = [[left[WROWS * i : WROWS * (i + 1), :]] for i in range(5)]
    for t in range(ncol):
        s = slice(t * LANES, (t + 1) * LANES)
        own = [r[:, s] for r in (rhs, lk, cr, cc, w)]
        rows = slice(MSG * t, MSG * (t + 1))
        for i, value in enumerate(windows(own, above[rows, :], below[rows, :])):
            pieces[i].append(value)
    for i in range(5):
        pieces[i].append(right[WROWS * i : WROWS * (i + 1), :])
    b, l, r, c, wt = [jnp.concatenate(p, axis=1) for p in pieces]
    n = b.shape[1]
    rw, cn = pltpu.roll(r, 1, 1), pltpu.roll(c, 1, 0)
    diag = l + r + c + rw + cn
    inside = l > 0.0
    inv = jnp.where(inside, 1.0 / jnp.where(inside, diag, 1.0), 0.0)
    east, west, south, north = r * inv, rw * inv, c * inv, cn * inv
    op = functools.partial(scaled_apply, east=east, west=west, south=south, north=north)
    z = b * inv
    d = z * (1.0 / THETA)
    x = d
    z = z - op(d)
    d = (RHO1 * RHO0) * d + (2.0 * RHO1 / DELTA) * z
    x = x + d
    z = z - op(d)
    d = (RHO2 * RHO1) * d + (2.0 * RHO2 / DELTA) * z
    x = x + d
    z = z - op(d)
    g = wt * diag * (z - OMEGA * op(z))
    pre_o[...] = x
    z_o[...] = z
    w_o[...] = wt
    east_o[...] = east
    west_o[...] = west
    south_o[...] = south
    north_o[...] = north
    part = g[8:16, LANES : 2 * LANES]
    for t in range(2, ncol + 1):
        part = part + g[8:16, t * LANES : (t + 1) * LANES]
    total = jnp.sum(part, axis=1, keepdims=True)
    place = (lax.axis_index("z") * 2 + lax.axis_index("core")) * 4
    lane = lax.broadcasted_iota(jnp.int32, (8, LANES), 1)
    row = lax.broadcasted_iota(jnp.int32, (8, LANES), 0)
    spread = jnp.where(lane == lax.rem(place, LANES) + row // 2, total, 0.0)
    line = jnp.sum(spread, axis=0, keepdims=True)
    rows = lax.broadcasted_iota(jnp.int32, (msg.shape[1], LANES), 0)
    msg[...] = jnp.broadcast_to(jnp.where(rows == place // LANES, line, 0.0)[None], msg.shape)


def last(xs, gathered, mflat, above, below, left, right, pre, z_i, wt, east, west, south, north, out):
    ncol = out.shape[1] // LANES
    ncols = lax.axis_size("cols")
    tiles = mflat.shape[0] // 4
    half = 2 * tiles
    at = 5 * WROWS
    own_m = [above[MSG * ncol + tiles * k : MSG * ncol + tiles * (k + 1), :] for k in range(2)]
    own_m += [mflat[tiles * k : tiles * (k + 1), :] for k in range(4)]
    own_m += [below[MSG * ncol + tiles * k : MSG * ncol + tiles * (k + 1), :] for k in range(2)]
    left_m = [left[at + tiles * k : at + tiles * (k + 1), :] for k in range(8)]
    right_m = [right[at + tiles * k : at + tiles * (k + 1), :] for k in range(8)]
    me = lax.axis_index("cols")
    blank = jnp.zeros((4, LANES), jnp.float32)

    def corrections(group, mats):
        v = []
        for x in range(xs):
            v.append(gathered[(2 * x) * ncols + group] + gathered[(2 * x + 1) * ncols + group])
        v = jnp.concatenate(v, axis=0)
        lines = [blank]
        for m in mats:
            p = jnp.sum(m * v, axis=0, keepdims=True)
            lines += [p, p]
        lines.append(blank)
        return jnp.sum(jnp.concatenate(lines, axis=0), axis=1, keepdims=True)

    cl = corrections(jnp.maximum(me - 1, 0), left_m)
    co = corrections(me, own_m)
    cn = corrections(jnp.minimum(me + 1, ncols - 1), right_m)
    w = wt[...]
    n = w.shape[1]
    lane = lax.broadcasted_iota(jnp.int32, (1, n), 1)
    lifted = w * jnp.where(lane < LANES, cl, jnp.where(lane >= n - LANES, cn, co))
    op = functools.partial(scaled_apply, east=east[...], west=west[...], south=south[...], north=north[...])
    e = lifted - OMEGA * op(lifted)
    x = pre[...] + e
    z = z_i[...] - op(e)
    d = z * (1.0 / THETA)
    x = x + d
    z = z - op(d)
    d = (RHO1 * RHO0) * d + (2.0 * RHO1 / DELTA) * z
    x = x + d
    z = z - op(d)
    d = (RHO2 * RHO1) * d + (2.0 * RHO2 / DELTA) * z
    x = x + d
    out[...] = x[8:16, LANES : n - LANES]


def local(sizes, rhs, cond_row, cond_col, leak, agg_members, coarse_inverse):
    xs, zs, cores, cols = sizes
    width = rhs.shape[1]
    ncol = width // LANES
    m = coarse_inverse[0]
    tiles = m.shape[1] // LANES
    group = agg_members.shape[2] // 4
    agg = agg_members[0, 0]
    length = MSG * ncol + 2 * tiles
    w, mflat, up, down = call(
        functools.partial(pack_rows, group),
        [f32(8, width), f32(4 * tiles, LANES), f32(length, LANES), f32(length, LANES)],
        6,
        "pack_rows",
    )(rhs, cond_row, cond_col, leak, agg, m)
    devices = xs * zs * cores
    ahead = [(i, i + 1) for i in range(devices - 1)]
    back = [(j, i) for i, j in ahead]
    above = lax.ppermute(down, ROWAX, ahead)
    below = lax.ppermute(up, ROWAX, back)
    edge = f32(5 * WROWS + 8 * tiles, LANES)
    to_left, to_right = call(pack_cols, [edge, edge], 8, "pack_cols")(
        rhs, cond_row, cond_col, leak, w, mflat, above, below
    )
    ahead = [(i, i + 1) for i in range(cols - 1)]
    back = [(j, i) for i, j in ahead]
    left = lax.ppermute(to_right, "cols", ahead)
    right = lax.ppermute(to_left, "cols", back)
    per_x = max(1, zs * cores * 4 // LANES)
    win = f32(WROWS, width + 2 * LANES)
    pre, z, wt, east, west, south, north, msg = call(
        functools.partial(middle, zs), [win] * 7 + [f32(zs, per_x, LANES)], 9, "middle"
    )(rhs, cond_row, cond_col, leak, w, above, below, left, right)
    got = lax.all_to_all(msg, "z", 0, 0, tiled=True)
    line = jnp.sum(got, axis=0)
    second = jnp.broadcast_to(line[None], (xs * cores * cols, per_x, LANES))
    gathered = lax.all_to_all(second, ("x", "core", "cols"), 0, 0, tiled=True)
    return call(functools.partial(last, xs), f32(8, width), 13, "last")(
        gathered, mflat, above, below, left, right, pre, z, wt, east, west, south, north
    )


def solution(mesh):
    rows, cols = mesh.shape["rows"], mesh.shape["cols"]
    cores = 2
    xs = 4 if rows == 256 else 2
    zs = rows // (xs * cores)
    fine = Mesh(mesh.devices.reshape(xs, zs, cores, cols), ("x", "z", "core", "cols"))
    spec = P(ROWAX, "cols")
    in_specs = (spec, spec, spec, spec, P(ROWAX, "cols", None, None), P("cols", ROWAX, None))
    return jax.shard_map(
        functools.partial(local, (xs, zs, cores, cols)),
        mesh=fine,
        in_specs=in_specs,
        out_specs=spec,
        check_vma=False,
    )
```

```python
import functools

import jax
import jax.numpy as jnp
from jax import lax
from jax.experimental import pallas as pl
from jax.experimental.pallas import tpu as pltpu
from jax.sharding import Mesh
from jax.sharding import PartitionSpec as P

THETA = 1.05
DELTA = 0.95
OMEGA = 2.0 / 3.0
RHO0 = DELTA / THETA
RHO1 = 1.0 / (2.0 * THETA / DELTA - RHO0)
RHO2 = 1.0 / (2.0 * THETA / DELTA - RHO1)
LANES = 128
REACH = 5
WROWS = 24
MSG = 24
ROWAX = ("x", "z", "core")
VMEM_LIMIT = 48 * 1024 * 1024
FIRST_LIMIT = 61 * 1024 * 1024


def call(kernel, outs, nin, name, space=pltpu.VMEM, scratch=(), limit=VMEM_LIMIT):
    return pl.pallas_call(
        kernel,
        out_shape=outs,
        in_specs=[pl.BlockSpec(memory_space=space)] * nin,
        out_specs=jax.tree.map(lambda _: pl.BlockSpec(memory_space=pltpu.VMEM), outs),
        scratch_shapes=scratch,
        compiler_params=pltpu.CompilerParams(vmem_limit_bytes=limit),
        name=name,
    )


def f32(*shape):
    return jax.ShapeDtypeStruct(shape, jnp.float32)


def weights(group, agg, w_ref):
    pairs = w_ref.shape[1] // 256
    per_row = 3 * pairs
    lane = lax.broadcasted_iota(jnp.int32, (8, LANES), 1)
    row = lax.broadcasted_iota(jnp.int32, (8, LANES), 0)
    for j in range(pairs):
        base = (row * pairs + j) * 256
        p1 = agg[pl.ds(3 * j + 1, 8, stride=per_row), :]
        p2 = agg[pl.ds(3 * j + 2, 8, stride=per_row), :]
        p1 = jnp.broadcast_to(p1[:, 0:1], (8, LANES)) - base
        p2 = jnp.broadcast_to(p2[:, 0:1], (8, LANES)) - base
        s0 = 1.0 / jnp.sqrt(p1.astype(jnp.float32) * float(group))
        s1 = 1.0 / jnp.sqrt((p2 - p1).astype(jnp.float32) * float(group))
        s2 = 1.0 / jnp.sqrt((256 - p2).astype(jnp.float32) * float(group))
        for half in range(2):
            at = lane + half * LANES
            value = jnp.where(at < p1, s0, jnp.where(at < p2, s1, s2))
            w_ref[:, (2 * j + half) * LANES : (2 * j + half + 1) * LANES] = value


def halo_rows(fields, downward):
    b, l, r, c, w = fields
    row = lax.broadcasted_iota(jnp.int32, (8, LANES), 0)
    first = jnp.concatenate([b[0:5], l[0:5], r[0:5], c[0:5], w[0:4]], axis=0)
    l = l + jnp.where(row == 3, pltpu.roll(c, 1, 0), 0.0)
    final = jnp.concatenate([b[3:8], l[3:8], r[3:8], c[3:8], w[4:8]], axis=0)
    return jnp.where(downward, final, first)


def first_kernel(group, rhs, cr, cc, lk, agg, m, w_o, mflat, core_msg, edges, b_v, r_v, c_v, l_v, agg_v, m_v, sems):
    copies = []
    for i, (src, dst) in enumerate(((agg, agg_v), (m, m_v), (rhs, b_v), (cr, r_v), (cc, c_v), (lk, l_v))):
        copies.append(pltpu.make_async_copy(src, dst, sems.at[i]))
    for copy in copies:
        copy.start()
    for copy in copies:
        copy.wait()
    weights(group, agg_v, w_o)
    tiles = m.shape[1] // LANES
    for k in range(4):
        for t in range(tiles):
            mflat[k * tiles + t : k * tiles + t + 1, :] = m_v[k : k + 1, t * LANES : (t + 1) * LANES]
    downward = lax.axis_index("core") == 0
    ncol = w_o.shape[1] // LANES
    refs = (b_v, l_v, r_v, c_v, w_o)
    for t in range(ncol):
        own = [r[:, t * LANES : (t + 1) * LANES] for r in refs]
        core_msg[MSG * t : MSG * (t + 1), :] = halo_rows(own, downward)
    half = 2 * tiles
    core_msg[MSG * ncol :, :] = jnp.where(downward, mflat[half:, :], mflat[:half, :])
    me = lax.axis_index("cols")
    cols = lax.axis_size("cols")
    n = w_o.shape[1]
    mine = mflat[...]
    left = jnp.concatenate([r[:, 0:LANES] for r in refs] + [mine], axis=0)
    right = jnp.concatenate([r[:, n - LANES : n] for r in refs] + [mine], axis=0)
    for c in range(cols):
        value = jnp.where(me > c, left, right)
        edges[c] = value
        edges[cols + c] = value


def side_block(got, core, step):
    cols = lax.axis_size("cols")
    c = lax.axis_index("cols") + step
    ok = jnp.logical_and(c >= 0, c < cols)
    return jnp.where(ok, got[core * cols + jnp.clip(c, 0, cols - 1)], 0.0)


def chip_kernel(b, r, c, l, w, mflat, got, s1, msg):
    core = lax.axis_index("core")
    downward = core == 1
    refs = (b, l, r, c, w)
    ncol = b.shape[1] // LANES
    half = mflat.shape[0] // 2
    lb, rb = side_block(got, core, -1), side_block(got, core, 1)
    columns = [[lb[8 * i : 8 * i + 8] for i in range(5)]]
    columns += [[x[:, t * LANES : (t + 1) * LANES] for x in refs] for t in range(ncol)]
    columns.append([rb[8 * i : 8 * i + 8] for i in range(5)])
    for t, fields in enumerate(columns):
        msg[MSG * t : MSG * (t + 1), :] = halo_rows(fields, downward)
    at = MSG * (ncol + 2)
    for i, mats in enumerate((lb[40:], mflat[...], rb[40:])):
        msg[at + half * i : at + half * (i + 1), :] = jnp.where(downward, mats[half:], mats[:half])


def unpacked(rows, top):
    out = []
    for i in range(5):
        n = 4 if i == 4 else REACH
        pad = jnp.zeros((8 - n, LANES), jnp.float32)
        piece = rows[5 * i : 5 * i + n]
        out.append(jnp.concatenate([pad, piece] if top else [piece, pad], axis=0))
    return out


def shifted(v):
    n = v.shape[1]
    r = v.shape[0]
    return (pltpu.roll(v, n - 1, 1), pltpu.roll(v, 1, 1), pltpu.roll(v, r - 1, 0), pltpu.roll(v, 1, 0))


def scaled_apply(v, east, west, south, north):
    e, w, s, n = shifted(v)
    return v - east * e - west * w - south * s - north * n


def middle(bf, rf, cf, lf, w, mflat, got, s1, s2, pre_o, z_o, w_o, east_o, west_o, south_o, north_o, mwin, msg):
    width = bf.shape[1]
    ncol = width // LANES
    core = lax.axis_index("core")
    upper = core == 0
    refs = (bf, lf, rf, cf, w)
    half = mflat.shape[0] // 2
    pieces = [[] for _ in range(5)]
    mats = []
    for t in range(ncol + 2):
        chip = s2[MSG * t : MSG * (t + 1), :]
        if 0 < t <= ncol:
            own = [x[:, (t - 1) * LANES : t * LANES] for x in refs]
            pair = s1[MSG * (t - 1) : MSG * t, :]
            above = unpacked(jnp.where(upper, chip, pair), True)
            below = unpacked(jnp.where(upper, pair, chip), False)
        else:
            step = -1 if t == 0 else 1
            block = side_block(got, core, step)
            pair = side_block(got, 1 - core, step)
            own = [block[8 * i : 8 * i + 8] for i in range(5)]
            near = [pair[8 * i : 8 * i + 8] for i in range(5)]
            above = [jnp.where(upper, a, e) for a, e in zip(unpacked(chip, True), near)]
            below = [jnp.where(upper, e, a) for a, e in zip(unpacked(chip, False), near)]
            mats.append((block[40:], jnp.where(upper, pair[40 : 40 + half], pair[40 + half :])))
        for i in range(5):
            pieces[i].append(jnp.concatenate([above[i], own[i], below[i]], axis=0))
    mats.insert(1, (mflat[...], s1[MSG * ncol :, :]))
    at = MSG * (ncol + 2)
    for i, (mine, pair) in enumerate(mats):
        chip = s2[at + half * i : at + half * (i + 1), :]
        mwin[4 * half * i : 4 * half * i + half, :] = jnp.where(upper, chip, pair)
        mwin[4 * half * i + half : 4 * half * i + 3 * half, :] = mine
        mwin[4 * half * i + 3 * half : 4 * half * (i + 1), :] = jnp.where(upper, pair, chip)
    b, l, r, c, wt = [jnp.concatenate(p, axis=1) for p in pieces]
    n = b.shape[1]
    rw, cn = pltpu.roll(r, 1, 1), pltpu.roll(c, 1, 0)
    diag = l + r + c + rw + cn
    inside = l > 0.0
    inv = jnp.where(inside, 1.0 / jnp.where(inside, diag, 1.0), 0.0)
    east, west, south, north = r * inv, rw * inv, c * inv, cn * inv
    op = functools.partial(scaled_apply, east=east, west=west, south=south, north=north)
    z = b * inv
    d = z * (1.0 / THETA)
    x = d
    z = z - op(d)
    d = (RHO1 * RHO0) * d + (2.0 * RHO1 / DELTA) * z
    x = x + d
    z = z - op(d)
    d = (RHO2 * RHO1) * d + (2.0 * RHO2 / DELTA) * z
    x = x + d
    z = z - op(d)
    g = wt * diag * (z - OMEGA * op(z))
    pre_o[...] = x
    z_o[...] = z
    w_o[...] = wt
    east_o[...] = east
    west_o[...] = west
    south_o[...] = south
    north_o[...] = north
    part = g[8:16, LANES : 2 * LANES]
    for t in range(2, ncol + 1):
        part = part + g[8:16, t * LANES : (t + 1) * LANES]
    total = jnp.sum(part, axis=1, keepdims=True)
    place = (lax.axis_index("z") * 2 + lax.axis_index("core")) * 4
    lane = lax.broadcasted_iota(jnp.int32, (8, LANES), 1)
    row = lax.broadcasted_iota(jnp.int32, (8, LANES), 0)
    spread = jnp.where(lane == lax.rem(place, LANES) + row // 2, total, 0.0)
    line = jnp.sum(spread, axis=0, keepdims=True)
    rows = lax.broadcasted_iota(jnp.int32, (msg.shape[1], LANES), 0)
    msg[...] = jnp.broadcast_to(jnp.where(rows == place // LANES, line, 0.0)[None], msg.shape)


def last(xs, gathered, mwin, pre, z_i, wt, east, west, south, north, out):
    ncols = lax.axis_size("cols")
    tiles = mwin.shape[0] // 24
    mats = [[mwin[tiles * (8 * g + k) : tiles * (8 * g + k + 1), :] for k in range(8)] for g in range(3)]
    me = lax.axis_index("cols")
    blank = jnp.zeros((4, LANES), jnp.float32)

    def corrections(group, mats):
        v = []
        for x in range(xs):
            v.append(gathered[(2 * x) * ncols + group] + gathered[(2 * x + 1) * ncols + group])
        v = jnp.concatenate(v, axis=0)
        lines = [blank]
        for m in mats:
            p = jnp.sum(m * v, axis=0, keepdims=True)
            lines += [p, p]
        lines.append(blank)
        return jnp.sum(jnp.concatenate(lines, axis=0), axis=1, keepdims=True)

    cl = corrections(jnp.maximum(me - 1, 0), mats[0])
    co = corrections(me, mats[1])
    cn = corrections(jnp.minimum(me + 1, ncols - 1), mats[2])
    w = wt[...]
    n = w.shape[1]
    lane = lax.broadcasted_iota(jnp.int32, (1, n), 1)
    lifted = w * jnp.where(lane < LANES, cl, jnp.where(lane >= n - LANES, cn, co))
    op = functools.partial(scaled_apply, east=east[...], west=west[...], south=south[...], north=north[...])
    e = lifted - OMEGA * op(lifted)
    x = pre[...] + e
    z = z_i[...] - op(e)
    d = z * (1.0 / THETA)
    x = x + d
    z = z - op(d)
    d = (RHO1 * RHO0) * d + (2.0 * RHO1 / DELTA) * z
    x = x + d
    z = z - op(d)
    d = (RHO2 * RHO1) * d + (2.0 * RHO2 / DELTA) * z
    x = x + d
    out[...] = x[8:16, LANES : n - LANES]


def local(sizes, rhs, cond_row, cond_col, leak, agg_members, coarse_inverse):
    xs, zs, cores, cols = sizes
    width = rhs.shape[1]
    ncol = width // LANES
    m = coarse_inverse[0]
    tiles = m.shape[1] // LANES
    group = agg_members.shape[2] // 4
    agg = agg_members[0, 0]
    block = f32(8, width)
    edge = 40 + 4 * tiles
    w, mflat, core_msg, edges = call(
        functools.partial(first_kernel, group),
        [block, f32(4 * tiles, LANES), f32(MSG * ncol + 2 * tiles, LANES), f32(cores * cols, edge, LANES)],
        6,
        "first",
        space=pltpu.HBM,
        limit=FIRST_LIMIT,
        scratch=[pltpu.VMEM((8, width), jnp.float32)] * 4
        + [
            pltpu.VMEM(agg.shape, jnp.int32),
            pltpu.VMEM(m.shape, jnp.float32),
            pltpu.SemaphoreType.DMA((6,)),
        ],
    )(rhs, cond_row, cond_col, leak, agg, m)
    b, r, c, l = rhs, cond_row, cond_col, leak
    s1 = lax.ppermute(core_msg, "core", [(0, 1), (1, 0)])
    got = lax.all_to_all(edges, ("core", "cols"), 0, 0, tiled=True)
    chip_msg = call(chip_kernel, f32(MSG * (ncol + 2) + 6 * tiles, LANES), 8, "chip")(
        b, r, c, l, w, mflat, got, s1
    )
    devices = xs * zs * cores
    swap = []
    for i in range(1, devices - 1, 2):
        swap += [(i, i + 1), (i + 1, i)]
    s2 = lax.ppermute(chip_msg, ROWAX, swap)
    per_x = max(1, zs * cores * 4 // LANES)
    win = f32(WROWS, width + 2 * LANES)
    pre, z, wt, east, west, south, north, mwin, msg = call(
        middle, [win] * 7 + [f32(24 * tiles, LANES), f32(zs, per_x, LANES)], 9, "middle"
    )(b, r, c, l, w, mflat, got, s1, s2)
    spread = lax.all_to_all(msg, "z", 0, 0, tiled=True)
    line = jnp.sum(spread, axis=0)
    second = jnp.broadcast_to(line[None], (xs * cores * cols, per_x, LANES))
    gathered = lax.all_to_all(second, ("x", "core", "cols"), 0, 0, tiled=True)
    return call(functools.partial(last, xs), block, 9, "last")(
        gathered, mwin, pre, z, wt, east, west, south, north
    )


def solution(mesh):
    rows, cols = mesh.shape["rows"], mesh.shape["cols"]
    cores = 2
    xs = 4 if rows == 256 else 2
    zs = rows // (xs * cores)
    fine = Mesh(mesh.devices.reshape(xs, zs, cores, cols), ("x", "z", "core", "cols"))
    spec = P(ROWAX, "cols")
    in_specs = (spec, spec, spec, spec, P(ROWAX, "cols", None, None), P("cols", ROWAX, None))
    return jax.shard_map(
        functools.partial(local, (xs, zs, cores, cols)),
        mesh=fine,
        in_specs=in_specs,
        out_specs=spec,
        check_vma=False,
    )
```

```python
import functools

import jax
import jax.numpy as jnp
from jax import lax
from jax.experimental import pallas as pl
from jax.experimental.pallas import tpu as pltpu
from jax.sharding import Mesh
from jax.sharding import PartitionSpec as P

THETA = 1.05
DELTA = 0.95
OMEGA = 2.0 / 3.0
RHO0 = DELTA / THETA
RHO1 = 1.0 / (2.0 * THETA / DELTA - RHO0)
RHO2 = 1.0 / (2.0 * THETA / DELTA - RHO1)
LANES = 128
HALO = 4
WROWS = 24
ROWAX = ("x", "z", "core")
VMEM_LIMIT = 48 * 1024 * 1024
FIRST_LIMIT = 61 * 1024 * 1024


def call(kernel, outs, nin, name, space=pltpu.VMEM, scratch=(), limit=VMEM_LIMIT):
    return pl.pallas_call(
        kernel,
        out_shape=outs,
        in_specs=[pl.BlockSpec(memory_space=space)] * nin,
        out_specs=jax.tree.map(lambda _: pl.BlockSpec(memory_space=pltpu.VMEM), outs),
        scratch_shapes=scratch,
        compiler_params=pltpu.CompilerParams(vmem_limit_bytes=limit),
        name=name,
    )


def f32(*shape):
    return jax.ShapeDtypeStruct(shape, jnp.float32)


def weights(group, agg, w_ref):
    pairs = w_ref.shape[1] // 256
    per_row = 3 * pairs
    lane = lax.broadcasted_iota(jnp.int32, (8, LANES), 1)
    row = lax.broadcasted_iota(jnp.int32, (8, LANES), 0)
    for j in range(pairs):
        base = (row * pairs + j) * 256
        p1 = agg[pl.ds(3 * j + 1, 8, stride=per_row), :]
        p2 = agg[pl.ds(3 * j + 2, 8, stride=per_row), :]
        p1 = jnp.broadcast_to(p1[:, 0:1], (8, LANES)) - base
        p2 = jnp.broadcast_to(p2[:, 0:1], (8, LANES)) - base
        s0 = 1.0 / jnp.sqrt(p1.astype(jnp.float32) * float(group))
        s1 = 1.0 / jnp.sqrt((p2 - p1).astype(jnp.float32) * float(group))
        s2 = 1.0 / jnp.sqrt((256 - p2).astype(jnp.float32) * float(group))
        for half in range(2):
            at = lane + half * LANES
            value = jnp.where(at < p1, s0, jnp.where(at < p2, s1, s2))
            w_ref[:, (2 * j + half) * LANES : (2 * j + half + 1) * LANES] = value


def first_kernel(group, rhs, cr, cc, lk, agg, m, w_o, mflat, edges, b_v, r_v, c_v, l_v, agg_v, m_v, sems):
    n = w_o.shape[1]
    copies = []
    for i, (src, dst) in enumerate(((agg, agg_v), (m, m_v), (rhs, b_v), (cr, r_v), (cc, c_v), (lk, l_v))):
        for at in (slice(0, LANES), slice(n - LANES, n)):
            if i < 2:
                copy = pltpu.make_async_copy(src, dst, sems.at[len(copies)])
            else:
                copy = pltpu.make_async_copy(src.at[:, at], dst.at[:, at], sems.at[len(copies)])
            copies.append(copy)
            if i < 2:
                break
    for copy in copies:
        copy.start()
    for copy in copies:
        copy.wait()
    weights(group, agg_v, w_o)
    tiles = m.shape[1] // LANES
    for k in range(4):
        for t in range(tiles):
            mflat[k * tiles + t : k * tiles + t + 1, :] = m_v[k : k + 1, t * LANES : (t + 1) * LANES]
    refs = (b_v, l_v, r_v, c_v, w_o)
    mine = mflat[...]
    left = jnp.concatenate([x[:, 0:LANES] for x in refs] + [mine], axis=0)
    right = jnp.concatenate([x[:, n - LANES : n] for x in refs] + [mine], axis=0)
    me = lax.axis_index("cols")
    for c in range(edges.shape[0]):
        edges[c] = jnp.where(me > c, left, right)


def side_block(got, step):
    cols = lax.axis_size("cols")
    c = lax.axis_index("cols") + step
    ok = jnp.logical_and(c >= 0, c < cols)
    return jnp.where(ok, got[jnp.clip(c, 0, cols - 1)], 0.0)


def widened(left, own, right):
    return jnp.concatenate([left, own, right], axis=1)


def halves(left, x, right, i):
    return widened(left[8 * i : 8 * i + 8], x[...], right[8 * i : 8 * i + 8])


def operator(l, r, c, inside):
    west, north = pltpu.roll(r, 1, 1), pltpu.roll(c, 1, 0)
    diag = l + r + c + west + north
    inv = jnp.where(inside, 1.0 / jnp.where(inside, diag, 1.0), 0.0)
    return diag, inv, (r * inv, west * inv, c * inv, north * inv)


def rows_kernel(b, r, c, l, got, core_msg, chip_msg):
    lower = lax.axis_index("core") == 1
    left, right = side_block(got, -1), side_block(got, 1)
    bw, lw, rw, cw = [halves(left, x, right, i) for i, x in enumerate((b, l, r, c))]
    _, inv, coef = operator(lw, rw, cw, lw > 0.0)
    z0 = bw * inv
    z1 = z0 - scaled_apply(z0 * (1.0 / THETA), *coef)
    row = lax.broadcasted_iota(jnp.int32, bw.shape, 0)
    far = jnp.logical_or(row == 3, row == 4)
    fields = (jnp.where(far, z0, bw), jnp.where(far, z1, lw), rw, cw)
    up = jnp.concatenate([x[0:4] for x in fields], axis=0)
    down = jnp.concatenate([x[4:8] for x in fields], axis=0)
    core_msg[...] = jnp.where(lower, up, down)
    chip_msg[...] = jnp.where(lower, down, up)


def share_kernel(w, mflat, got, core_late, chip_late):
    lower = lax.axis_index("core") == 1
    left, right = side_block(got, -1), side_block(got, 1)
    ww = halves(left, w, right, 4)
    half = mflat.shape[0] // 2
    mats = (left[40:], mflat[...], right[40:])
    ncol = ww.shape[1] // LANES
    late_up = [ww[0:4, t * LANES : (t + 1) * LANES] for t in range(ncol)] + [x[:half] for x in mats]
    late_down = [ww[4:8, t * LANES : (t + 1) * LANES] for t in range(ncol)] + [x[half:] for x in mats]
    late_up, late_down = jnp.concatenate(late_up, axis=0), jnp.concatenate(late_down, axis=0)
    core_late[...] = jnp.where(lower, late_up, late_down)
    chip_late[...] = jnp.where(lower, late_down, late_up)


def shifted(v):
    n = v.shape[1]
    r = v.shape[0]
    return (pltpu.roll(v, n - 1, 1), pltpu.roll(v, 1, 1), pltpu.roll(v, r - 1, 0), pltpu.roll(v, 1, 0))


def scaled_apply(v, east, west, south, north):
    e, w, s, n = shifted(v)
    return v - east * e - west * w - south * s - north * n


def middle(b, r, c, l, w, got, s2, s1, pre_o, z_o, east_o, west_o, south_o, north_o, msg):
    upper = lax.axis_index("core") == 0
    left, right = side_block(got, -1), side_block(got, 1)
    pair, chip = s1[...], s2[...]
    above, below = jnp.where(upper, chip, pair), jnp.where(upper, pair, chip)
    pad = jnp.zeros((8 - HALO, above.shape[1]), jnp.float32)
    wins = []
    for i, x in enumerate((b, l, r, c)):
        at = slice(HALO * i, HALO * (i + 1))
        wins.append(jnp.concatenate([pad, above[at], halves(left, x, right, i), below[at], pad], axis=0))
    bw, lw, rw, cw = wins
    n = bw.shape[1]
    ncol = n // LANES - 2
    row = lax.broadcasted_iota(jnp.int32, bw.shape, 0)
    far = jnp.logical_or(row == 4, row == 19)
    inside = jnp.logical_and(lw > 0.0, jnp.logical_not(far))
    diag, inv, coef = operator(lw, rw, cw, inside)
    z = jnp.where(far, bw, bw * inv)
    d = z * (1.0 / THETA)
    x = d
    z = jnp.where(far, lw, z - scaled_apply(d, *coef))
    d = (RHO1 * RHO0) * d + (2.0 * RHO1 / DELTA) * z
    x = x + d
    z = z - scaled_apply(d, *coef)
    d = (RHO2 * RHO1) * d + (2.0 * RHO2 / DELTA) * z
    x = x + d
    z = z - scaled_apply(d, *coef)
    own = slice(8, 16)
    g = diag[own] * (z - OMEGA * scaled_apply(z, *coef))[own]
    part = jnp.zeros((8, LANES), jnp.float32)
    for t in range(ncol):
        part = part + w[:, t * LANES : (t + 1) * LANES] * g[:, (t + 1) * LANES : (t + 2) * LANES]
    pre_o[...] = x
    z_o[...] = z
    for ref, value in zip((east_o, west_o, south_o, north_o), coef):
        ref[...] = value
    total = jnp.sum(part, axis=1, keepdims=True)
    place = (lax.axis_index("z") * 2 + lax.axis_index("core")) * 4
    lane = lax.broadcasted_iota(jnp.int32, (8, LANES), 1)
    row = lax.broadcasted_iota(jnp.int32, (8, LANES), 0)
    spread = jnp.where(lane == lax.rem(place, LANES) + row // 2, total, 0.0)
    line = jnp.sum(spread, axis=0, keepdims=True)
    rows = lax.broadcasted_iota(jnp.int32, (msg.shape[1], LANES), 0)
    msg[...] = jnp.broadcast_to(jnp.where(rows == place // LANES, line, 0.0)[None], msg.shape)


def late_kernel(w, mflat, got, s1, s2, wt, mwin):
    upper = lax.axis_index("core") == 0
    left, right = side_block(got, -1), side_block(got, 1)
    pair, chip = s1[...], s2[...]
    above, below = jnp.where(upper, chip, pair), jnp.where(upper, pair, chip)
    ww = halves(left, w, right, 4)
    ncol = ww.shape[1] // LANES
    pad = jnp.zeros((8 - HALO, LANES), jnp.float32)
    for t in range(ncol):
        at = slice(HALO * t, HALO * (t + 1))
        s = slice(t * LANES, (t + 1) * LANES)
        wt[:, s] = jnp.concatenate([pad, above[at], ww[:, s], below[at], pad], axis=0)
    half = mflat.shape[0] // 2
    for i, mine in enumerate((left[40:], mflat[...], right[40:])):
        at = slice(HALO * ncol + half * i, HALO * ncol + half * (i + 1))
        mwin[4 * half * i : 4 * half * i + half, :] = above[at]
        mwin[4 * half * i + half : 4 * half * i + 3 * half, :] = mine
        mwin[4 * half * i + 3 * half : 4 * half * (i + 1), :] = below[at]


def last(xs, gathered, mwin, pre, z_i, wt, east, west, south, north, out):
    ncols = lax.axis_size("cols")
    tiles = mwin.shape[0] // 24
    mats = [[mwin[tiles * (8 * g + k) : tiles * (8 * g + k + 1), :] for k in range(8)] for g in range(3)]
    me = lax.axis_index("cols")
    blank = jnp.zeros((4, LANES), jnp.float32)

    def corrections(group, mats):
        v = []
        for x in range(xs):
            v.append(gathered[(2 * x) * ncols + group] + gathered[(2 * x + 1) * ncols + group])
        v = jnp.concatenate(v, axis=0)
        lines = [blank]
        for m in mats:
            p = jnp.sum(m * v, axis=0, keepdims=True)
            lines += [p, p]
        lines.append(blank)
        return jnp.sum(jnp.concatenate(lines, axis=0), axis=1, keepdims=True)

    cl = corrections(jnp.maximum(me - 1, 0), mats[0])
    co = corrections(me, mats[1])
    cn = corrections(jnp.minimum(me + 1, ncols - 1), mats[2])
    w = wt[...]
    n = w.shape[1]
    lane = lax.broadcasted_iota(jnp.int32, (1, n), 1)
    lifted = w * jnp.where(lane < LANES, cl, jnp.where(lane >= n - LANES, cn, co))
    op = functools.partial(scaled_apply, east=east[...], west=west[...], south=south[...], north=north[...])
    e = lifted - OMEGA * op(lifted)
    x = pre[...] + e
    z = z_i[...] - op(e)
    d = z * (1.0 / THETA)
    x = x + d
    z = z - op(d)
    d = (RHO1 * RHO0) * d + (2.0 * RHO1 / DELTA) * z
    x = x + d
    z = z - op(d)
    d = (RHO2 * RHO1) * d + (2.0 * RHO2 / DELTA) * z
    x = x + d
    out[...] = x[8:16, LANES : n - LANES]


def local(sizes, rhs, cond_row, cond_col, leak, agg_members, coarse_inverse):
    xs, zs, cores, cols = sizes
    width = rhs.shape[1]
    wide = width + 2 * LANES
    m = coarse_inverse[0]
    tiles = m.shape[1] // LANES
    group = agg_members.shape[2] // 4
    agg = agg_members[0, 0]
    block = f32(8, width)
    w, mflat, edges = call(
        functools.partial(first_kernel, group),
        [block, f32(4 * tiles, LANES), f32(cols, 40 + 4 * tiles, LANES)],
        6,
        "first",
        space=pltpu.HBM,
        limit=FIRST_LIMIT,
        scratch=[pltpu.VMEM((8, width), jnp.float32)] * 4
        + [
            pltpu.VMEM(agg.shape, jnp.int32),
            pltpu.VMEM(m.shape, jnp.float32),
            pltpu.SemaphoreType.DMA((10,)),
        ],
    )(rhs, cond_row, cond_col, leak, agg, m)
    b, r, c, l = rhs, cond_row, cond_col, leak
    got = lax.all_to_all(edges, "cols", 0, 0, tiled=True)
    message = f32(4 * HALO, wide)
    late = f32(HALO * wide // LANES + 6 * tiles, LANES)
    devices = xs * zs * cores
    swap = []
    for i in range(1, devices - 1, 2):
        swap += [(i, i + 1), (i + 1, i)]
    core_msg, chip_msg = call(rows_kernel, [message, message], 5, "rows")(b, r, c, l, got)
    s2 = lax.ppermute(chip_msg, ROWAX, swap)
    s1 = lax.ppermute(core_msg, "core", [(0, 1), (1, 0)])
    per_x = max(1, zs * cores * 4 // LANES)
    win = f32(WROWS, wide)
    pre, z, east, west, south, north, msg = call(middle, [win] * 6 + [f32(zs, per_x, LANES)], 8, "middle")(
        b, r, c, l, w, got, s2, s1
    )
    spread = lax.all_to_all(msg, "z", 0, 0, tiled=True)
    core_late, chip_late = call(share_kernel, [late, late], 3, "share")(w, mflat, got)
    s2_late = lax.ppermute(chip_late, ROWAX, swap)
    s1_late = lax.ppermute(core_late, "core", [(0, 1), (1, 0)])
    wt, mwin = call(late_kernel, [win, f32(24 * tiles, LANES)], 5, "late")(w, mflat, got, s1_late, s2_late)
    line = jnp.sum(spread, axis=0)
    second = jnp.broadcast_to(line[None], (xs * cores * cols, per_x, LANES))
    gathered = lax.all_to_all(second, ("x", "core", "cols"), 0, 0, tiled=True)
    return call(functools.partial(last, xs), block, 9, "last")(
        gathered, mwin, pre, z, wt, east, west, south, north
    )


def solution(mesh):
    rows, cols = mesh.shape["rows"], mesh.shape["cols"]
    cores = 2
    xs = 4 if rows == 256 else 2
    zs = rows // (xs * cores)
    fine = Mesh(mesh.devices.reshape(xs, zs, cores, cols), ("x", "z", "core", "cols"))
    spec = P(ROWAX, "cols")
    in_specs = (spec, spec, spec, spec, P(ROWAX, "cols", None, None), P("cols", ROWAX, None))
    return jax.shard_map(
        functools.partial(local, (xs, zs, cores, cols)),
        mesh=fine,
        in_specs=in_specs,
        out_specs=spec,
        check_vma=False,
    )
```

```python
import functools

import jax
import jax.numpy as jnp
from jax import lax
from jax.experimental import pallas as pl
from jax.experimental.pallas import tpu as pltpu
from jax.sharding import Mesh
from jax.sharding import PartitionSpec as P

THETA = 1.05
DELTA = 0.95
OMEGA = 2.0 / 3.0
RHO0 = DELTA / THETA
RHO1 = 1.0 / (2.0 * THETA / DELTA - RHO0)
RHO2 = 1.0 / (2.0 * THETA / DELTA - RHO1)
LANES = 128
HALO = 4
WROWS = 16
ROWAX = ("x", "z", "core")
VMEM_LIMIT = 48 * 1024 * 1024
FIRST_LIMIT = 61 * 1024 * 1024


def call(kernel, outs, nin, name, space=pltpu.VMEM, scratch=(), limit=VMEM_LIMIT):
    return pl.pallas_call(
        kernel,
        out_shape=outs,
        in_specs=[pl.BlockSpec(memory_space=space)] * nin,
        out_specs=jax.tree.map(lambda _: pl.BlockSpec(memory_space=pltpu.VMEM), outs),
        scratch_shapes=scratch,
        compiler_params=pltpu.CompilerParams(vmem_limit_bytes=limit),
        name=name,
    )


def f32(*shape):
    return jax.ShapeDtypeStruct(shape, jnp.float32)


def weights(group, agg, w_ref):
    pairs = w_ref.shape[1] // 256
    per_row = 3 * pairs
    lane = lax.broadcasted_iota(jnp.int32, (8, LANES), 1)
    row = lax.broadcasted_iota(jnp.int32, (8, LANES), 0)
    for j in range(pairs):
        base = (row * pairs + j) * 256
        p1 = agg[pl.ds(3 * j + 1, 8, stride=per_row), :]
        p2 = agg[pl.ds(3 * j + 2, 8, stride=per_row), :]
        p1 = jnp.broadcast_to(p1[:, 0:1], (8, LANES)) - base
        p2 = jnp.broadcast_to(p2[:, 0:1], (8, LANES)) - base
        s0 = 1.0 / jnp.sqrt(p1.astype(jnp.float32) * float(group))
        s1 = 1.0 / jnp.sqrt((p2 - p1).astype(jnp.float32) * float(group))
        s2 = 1.0 / jnp.sqrt((256 - p2).astype(jnp.float32) * float(group))
        for half in range(2):
            at = lane + half * LANES
            value = jnp.where(at < p1, s0, jnp.where(at < p2, s1, s2))
            w_ref[:, (2 * j + half) * LANES : (2 * j + half + 1) * LANES] = value


def flatten(m, mflat):
    tiles = m.shape[1] // LANES
    for k in range(4):
        for t in range(tiles):
            mflat[k * tiles + t : k * tiles + t + 1, :] = m[k : k + 1, t * LANES : (t + 1) * LANES]


def first_kernel(group, rhs, cr, cc, lk, agg, m, edges, b_v, r_v, c_v, l_v, agg_v, m_v, w_v, mflat, sems):
    n = w_v.shape[1]
    copies = []
    for i, (src, dst) in enumerate(((agg, agg_v), (m, m_v), (rhs, b_v), (cr, r_v), (cc, c_v), (lk, l_v))):
        for at in (slice(0, LANES), slice(n - LANES, n)):
            if i < 2:
                copy = pltpu.make_async_copy(src, dst, sems.at[len(copies)])
            else:
                copy = pltpu.make_async_copy(src.at[:, at], dst.at[:, at], sems.at[len(copies)])
            copies.append(copy)
            if i < 2:
                break
    for copy in copies:
        copy.start()
    for copy in copies:
        copy.wait()
    weights(group, agg_v, w_v)
    flatten(m_v, mflat)
    refs = (b_v, l_v, r_v, c_v, w_v)
    mine = mflat[...]
    left = jnp.concatenate([x[:, 0:LANES] for x in refs] + [mine], axis=0)
    right = jnp.concatenate([x[:, n - LANES : n] for x in refs] + [mine], axis=0)
    me = lax.axis_index("cols")
    for c in range(edges.shape[0]):
        edges[c] = jnp.where(me > c, left, right)


def side_block(got, step):
    cols = lax.axis_size("cols")
    c = lax.axis_index("cols") + step
    ok = jnp.logical_and(c >= 0, c < cols)
    return jnp.where(ok, got[jnp.clip(c, 0, cols - 1)], 0.0)


def widened(left, own, right):
    return jnp.concatenate([left, own, right], axis=1)


def halves(left, x, right, i):
    return widened(left[8 * i : 8 * i + 8], x[...], right[8 * i : 8 * i + 8])


def operator(l, r, c, inside):
    west, north = pltpu.roll(r, 1, 1), pltpu.roll(c, 1, 0)
    diag = l + r + c + west + north
    inv = jnp.where(inside, 1.0 / jnp.where(inside, diag, 1.0), 0.0)
    return diag, inv, (r * inv, west * inv, c * inv, north * inv)


def row_messages(b, r, c, l, left, right):
    bw, lw, rw, cw = [halves(left, x, right, i) for i, x in enumerate((b, l, r, c))]
    _, inv, coef = operator(lw, rw, cw, lw > 0.0)
    z0 = bw * inv
    z1 = z0 - scaled_apply(z0 * (1.0 / THETA), *coef)
    row = lax.broadcasted_iota(jnp.int32, bw.shape, 0)
    far = jnp.logical_or(row == 3, row == 4)
    fields = (jnp.where(far, z0, bw), jnp.where(far, z1, lw), rw, cw)
    up = jnp.concatenate([x[0:4] for x in fields], axis=0)
    down = jnp.concatenate([x[4:8] for x in fields], axis=0)
    return up, down


def rows_kernel(group, b, r, c, l, agg, m, got, chip_msg, core_msg, chip_late, w, mflat):
    weights(group, agg, w)
    flatten(m, mflat)
    lower = lax.axis_index("core") == 1
    left, right = side_block(got, -1), side_block(got, 1)
    up, down = row_messages(b, r, c, l, left, right)
    chip_msg[...] = jnp.where(lower, down, up)
    message = jnp.where(lower, up, down)
    ww = halves(left, w, right, 4)
    half = mflat.shape[0] // 2
    mats = (left[40:], mflat[...], right[40:])
    ncol = ww.shape[1] // LANES
    rows = 4 * HALO
    for t in range(ncol):
        core_msg[rows * t : rows * (t + 1), :] = message[:, t * LANES : (t + 1) * LANES]
    late_up = [ww[0:4, t * LANES : (t + 1) * LANES] for t in range(ncol)] + [x[:half] for x in mats]
    late_down = [ww[4:8, t * LANES : (t + 1) * LANES] for t in range(ncol)] + [x[half:] for x in mats]
    late_up, late_down = jnp.concatenate(late_up, axis=0), jnp.concatenate(late_down, axis=0)
    core_msg[rows * ncol :, :] = jnp.where(lower, late_up, late_down)
    chip_late[...] = jnp.where(lower, late_down, late_up)


def shifted(v):
    n = v.shape[1]
    r = v.shape[0]
    return (pltpu.roll(v, n - 1, 1), pltpu.roll(v, 1, 1), pltpu.roll(v, r - 1, 0), pltpu.roll(v, 1, 0))


def scaled_apply(v, east, west, south, north):
    e, w, s, n = shifted(v)
    return v - east * e - west * w - south * s - north * n


def middle(b, r, c, l, w, got, s2, s1, pre_o, z_o, east_o, west_o, south_o, north_o, msg):
    upper = lax.axis_index("core") == 0
    left, right = side_block(got, -1), side_block(got, 1)
    chip = s2[...]
    rows = 4 * HALO
    pair = jnp.concatenate([s1[rows * t : rows * (t + 1), :] for t in range(chip.shape[1] // LANES)], axis=1)
    above, below = jnp.where(upper, chip, pair), jnp.where(upper, pair, chip)
    wins = []
    for i, x in enumerate((b, l, r, c)):
        at = slice(HALO * i, HALO * (i + 1))
        wins.append(jnp.concatenate([halves(left, x, right, i), below[at], above[at]], axis=0))
    bw, lw, rw, cw = wins
    n = bw.shape[1]
    ncol = n // LANES - 2
    row = lax.broadcasted_iota(jnp.int32, bw.shape, 0)
    far = jnp.logical_or(row == 11, row == 12)
    inside = jnp.logical_and(lw > 0.0, jnp.logical_not(far))
    diag, inv, coef = operator(lw, rw, cw, inside)
    z = jnp.where(far, bw, bw * inv)
    d = z * (1.0 / THETA)
    x = d
    z = jnp.where(far, lw, z - scaled_apply(d, *coef))
    d = (RHO1 * RHO0) * d + (2.0 * RHO1 / DELTA) * z
    x = x + d
    z = z - scaled_apply(d, *coef)
    d = (RHO2 * RHO1) * d + (2.0 * RHO2 / DELTA) * z
    x = x + d
    z = z - scaled_apply(d, *coef)
    own = slice(0, 8)
    g = diag[own] * (z - OMEGA * scaled_apply(z, *coef))[own]
    part = jnp.zeros((8, LANES), jnp.float32)
    for t in range(ncol):
        part = part + w[:, t * LANES : (t + 1) * LANES] * g[:, (t + 1) * LANES : (t + 2) * LANES]
    pre_o[...] = x
    z_o[...] = z
    for ref, value in zip((east_o, west_o, south_o, north_o), coef):
        ref[...] = value
    total = jnp.sum(part, axis=1, keepdims=True)
    place = (lax.axis_index("z") * 2 + lax.axis_index("core")) * 4
    lane = lax.broadcasted_iota(jnp.int32, (8, LANES), 1)
    row = lax.broadcasted_iota(jnp.int32, (8, LANES), 0)
    spread = jnp.where(lane == lax.rem(place, LANES) + row // 2, total, 0.0)
    line = jnp.sum(spread, axis=0, keepdims=True)
    rows = lax.broadcasted_iota(jnp.int32, (msg.shape[1], LANES), 0)
    msg[...] = jnp.broadcast_to(jnp.where(rows == place // LANES, line, 0.0)[None], msg.shape)


def late_kernel(w, mflat, got, s1, s2, wt, mwin):
    upper = lax.axis_index("core") == 0
    left, right = side_block(got, -1), side_block(got, 1)
    pair, chip = s1[s1.shape[0] - s2.shape[0] :, :], s2[...]
    above, below = jnp.where(upper, chip, pair), jnp.where(upper, pair, chip)
    ww = halves(left, w, right, 4)
    ncol = ww.shape[1] // LANES
    for t in range(ncol):
        at = slice(HALO * t, HALO * (t + 1))
        s = slice(t * LANES, (t + 1) * LANES)
        wt[:, s] = jnp.concatenate([ww[:, s], below[at], above[at]], axis=0)
    half = mflat.shape[0] // 2
    for i, mine in enumerate((left[40:], mflat[...], right[40:])):
        at = slice(HALO * ncol + half * i, HALO * ncol + half * (i + 1))
        mwin[4 * half * i : 4 * half * i + half, :] = above[at]
        mwin[4 * half * i + half : 4 * half * i + 3 * half, :] = mine
        mwin[4 * half * i + 3 * half : 4 * half * (i + 1), :] = below[at]


def last(xs, gathered, mwin, pre, z_i, wt, east, west, south, north, out):
    ncols = lax.axis_size("cols")
    tiles = mwin.shape[0] // 24
    mats = [[mwin[tiles * (8 * g + k) : tiles * (8 * g + k + 1), :] for k in range(8)] for g in range(3)]
    me = lax.axis_index("cols")

    def corrections(group, mats):
        v = []
        for x in range(xs):
            v.append(gathered[(2 * x) * ncols + group] + gathered[(2 * x + 1) * ncols + group])
        v = jnp.concatenate(v, axis=0)
        lines = []
        for m in mats[2:] + mats[:2]:
            p = jnp.sum(m * v, axis=0, keepdims=True)
            lines += [p, p]
        return jnp.sum(jnp.concatenate(lines, axis=0), axis=1, keepdims=True)

    cl = corrections(jnp.maximum(me - 1, 0), mats[0])
    co = corrections(me, mats[1])
    cn = corrections(jnp.minimum(me + 1, ncols - 1), mats[2])
    w = wt[...]
    n = w.shape[1]
    lane = lax.broadcasted_iota(jnp.int32, (1, n), 1)
    lifted = w * jnp.where(lane < LANES, cl, jnp.where(lane >= n - LANES, cn, co))
    op = functools.partial(scaled_apply, east=east[...], west=west[...], south=south[...], north=north[...])
    e = lifted - OMEGA * op(lifted)
    x = pre[...] + e
    z = z_i[...] - op(e)
    d = z * (1.0 / THETA)
    x = x + d
    z = z - op(d)
    d = (RHO1 * RHO0) * d + (2.0 * RHO1 / DELTA) * z
    x = x + d
    z = z - op(d)
    d = (RHO2 * RHO1) * d + (2.0 * RHO2 / DELTA) * z
    x = x + d
    out[...] = x[0:8, LANES : n - LANES]


def local(sizes, rhs, cond_row, cond_col, leak, agg_members, coarse_inverse):
    xs, zs, cores, cols = sizes
    width = rhs.shape[1]
    wide = width + 2 * LANES
    m = coarse_inverse[0]
    tiles = m.shape[1] // LANES
    group = agg_members.shape[2] // 4
    agg = agg_members[0, 0]
    block = f32(8, width)
    edges = call(
        functools.partial(first_kernel, group),
        f32(cols, 40 + 4 * tiles, LANES),
        6,
        "first",
        space=pltpu.HBM,
        limit=FIRST_LIMIT,
        scratch=[pltpu.VMEM((8, width), jnp.float32)] * 4
        + [
            pltpu.VMEM(agg.shape, jnp.int32),
            pltpu.VMEM(m.shape, jnp.float32),
            pltpu.VMEM((8, width), jnp.float32),
            pltpu.VMEM((4 * tiles, LANES), jnp.float32),
            pltpu.SemaphoreType.DMA((10,)),
        ],
    )(rhs, cond_row, cond_col, leak, agg, m)
    b, r, c, l = rhs, cond_row, cond_col, leak
    got = lax.all_to_all(edges, "cols", 0, 0, tiled=True)
    devices = xs * zs * cores
    swap = []
    for i in range(1, devices - 1, 2):
        swap += [(i, i + 1), (i + 1, i)]
    late = HALO * wide // LANES + 6 * tiles
    chip_msg, core_msg, chip_late, w, mflat = call(
        functools.partial(rows_kernel, group),
        [f32(4 * HALO, wide), f32(4 * HALO * wide // LANES + late, LANES), f32(late, LANES), block, f32(4 * tiles, LANES)],
        7,
        "rows",
    )(b, r, c, l, agg, m, got)
    s2 = lax.ppermute(chip_msg, ROWAX, swap)
    s1 = lax.ppermute(core_msg, "core", [(0, 1), (1, 0)])
    per_x = max(1, zs * cores * 4 // LANES)
    win = f32(WROWS, wide)
    pre, z, east, west, south, north, msg = call(middle, [win] * 6 + [f32(zs, per_x, LANES)], 8, "middle")(
        b, r, c, l, w, got, s2, s1
    )
    spread = lax.all_to_all(msg, "z", 0, 0, tiled=True)
    s2_late = lax.ppermute(chip_late, ROWAX, swap)
    wt, mwin = call(late_kernel, [win, f32(24 * tiles, LANES)], 5, "late")(w, mflat, got, s1, s2_late)
    line = jnp.sum(spread, axis=0)
    second = jnp.broadcast_to(line[None], (xs * cores * cols, per_x, LANES))
    gathered = lax.all_to_all(second, ("x", "core", "cols"), 0, 0, tiled=True)
    return call(functools.partial(last, xs), block, 9, "last")(
        gathered, mwin, pre, z, wt, east, west, south, north
    )


def solution(mesh):
    rows, cols = mesh.shape["rows"], mesh.shape["cols"]
    cores = 2
    xs = 4 if rows == 256 else 2
    zs = rows // (xs * cores)
    fine = Mesh(mesh.devices.reshape(xs, zs, cores, cols), ("x", "z", "core", "cols"))
    spec = P(ROWAX, "cols")
    in_specs = (spec, spec, spec, spec, P(ROWAX, "cols", None, None), P("cols", ROWAX, None))
    return jax.shard_map(
        functools.partial(local, (xs, zs, cores, cols)),
        mesh=fine,
        in_specs=in_specs,
        out_specs=spec,
        check_vma=False,
    )
```

```python
import functools

import jax
import jax.numpy as jnp
from jax import lax
from jax.experimental import pallas as pl
from jax.experimental.pallas import tpu as pltpu
from jax.sharding import Mesh
from jax.sharding import PartitionSpec as P

THETA = 1.05
DELTA = 0.95
OMEGA = 2.0 / 3.0
RHO0 = DELTA / THETA
RHO1 = 1.0 / (2.0 * THETA / DELTA - RHO0)
RHO2 = 1.0 / (2.0 * THETA / DELTA - RHO1)
LANES = 128
HALO = 4
WROWS = 16
ROWAX = ("x", "z", "core")
VMEM_LIMIT = 48 * 1024 * 1024
FIRST_LIMIT = 61 * 1024 * 1024


def call(kernel, outs, nin, name, space=pltpu.VMEM, scratch=(), limit=VMEM_LIMIT):
    return pl.pallas_call(
        kernel,
        out_shape=outs,
        in_specs=[pl.BlockSpec(memory_space=space)] * nin,
        out_specs=jax.tree.map(lambda _: pl.BlockSpec(memory_space=pltpu.VMEM), outs),
        scratch_shapes=scratch,
        compiler_params=pltpu.CompilerParams(vmem_limit_bytes=limit),
        name=name,
    )


def f32(*shape):
    return jax.ShapeDtypeStruct(shape, jnp.float32)


def weights(group, agg, w_ref):
    pairs = w_ref.shape[1] // 256
    per_row = 3 * pairs
    lane = lax.broadcasted_iota(jnp.int32, (8, LANES), 1)
    row = lax.broadcasted_iota(jnp.int32, (8, LANES), 0)
    for j in range(pairs):
        base = (row * pairs + j) * 256
        p1 = agg[pl.ds(3 * j + 1, 8, stride=per_row), :]
        p2 = agg[pl.ds(3 * j + 2, 8, stride=per_row), :]
        p1 = jnp.broadcast_to(p1[:, 0:1], (8, LANES)) - base
        p2 = jnp.broadcast_to(p2[:, 0:1], (8, LANES)) - base
        s0 = 1.0 / jnp.sqrt(p1.astype(jnp.float32) * float(group))
        s1 = 1.0 / jnp.sqrt((p2 - p1).astype(jnp.float32) * float(group))
        s2 = 1.0 / jnp.sqrt((256 - p2).astype(jnp.float32) * float(group))
        for half in range(2):
            at = lane + half * LANES
            value = jnp.where(at < p1, s0, jnp.where(at < p2, s1, s2))
            w_ref[:, (2 * j + half) * LANES : (2 * j + half + 1) * LANES] = value


def flatten(m, mflat):
    tiles = m.shape[1] // LANES
    for k in range(4):
        for t in range(tiles):
            mflat[k * tiles + t : k * tiles + t + 1, :] = m[k : k + 1, t * LANES : (t + 1) * LANES]


def first_kernel(group, rhs, cr, cc, lk, agg, m, edges, b_v, r_v, c_v, l_v, agg_v, m_v, w_v, mflat, sems):
    n = w_v.shape[1]
    copies = []
    for i, (src, dst) in enumerate(((agg, agg_v), (m, m_v), (rhs, b_v), (cr, r_v), (cc, c_v), (lk, l_v))):
        for at in (slice(0, LANES), slice(n - LANES, n)):
            if i < 2:
                copy = pltpu.make_async_copy(src, dst, sems.at[len(copies)])
            else:
                copy = pltpu.make_async_copy(src.at[:, at], dst.at[:, at], sems.at[len(copies)])
            copies.append(copy)
            if i < 2:
                break
    for copy in copies:
        copy.start()
    for copy in copies:
        copy.wait()
    weights(group, agg_v, w_v)
    flatten(m_v, mflat)
    refs = (b_v, l_v, r_v, c_v, w_v)
    mine = mflat[...]
    left = jnp.concatenate([x[:, 0:LANES] for x in refs] + [mine], axis=0)
    right = jnp.concatenate([x[:, n - LANES : n] for x in refs] + [mine], axis=0)
    me = lax.axis_index("cols")
    for c in range(edges.shape[0]):
        edges[c] = jnp.where(me > c, left, right)


def side_block(got, step):
    cols = lax.axis_size("cols")
    c = lax.axis_index("cols") + step
    ok = jnp.logical_and(c >= 0, c < cols)
    return jnp.where(ok, got[jnp.clip(c, 0, cols - 1)], 0.0)


def widened(left, own, right):
    return jnp.concatenate([left, own, right], axis=1)


def halves(left, x, right, i):
    return widened(left[8 * i : 8 * i + 8], x[...], right[8 * i : 8 * i + 8])


def operator(l, r, c, inside):
    west, north = pltpu.roll(r, 1, 1), pltpu.roll(c, 1, 0)
    diag = l + r + c + west + north
    inv = jnp.where(inside, 1.0 / jnp.where(inside, diag, 1.0), 0.0)
    return diag, inv, (r * inv, west * inv, c * inv, north * inv)


def row_messages(b, r, c, l, left, right):
    bw, lw, rw, cw = [halves(left, x, right, i) for i, x in enumerate((b, l, r, c))]
    _, inv, coef = operator(lw, rw, cw, lw > 0.0)
    z0 = bw * inv
    z1 = z0 - scaled_apply(z0 * (1.0 / THETA), *coef)
    row = lax.broadcasted_iota(jnp.int32, bw.shape, 0)
    far = jnp.logical_or(row == 3, row == 4)
    fields = (jnp.where(far, z0, bw), jnp.where(far, z1, lw), rw, cw)
    up = jnp.concatenate([x[0:4] for x in fields], axis=0)
    down = jnp.concatenate([x[4:8] for x in fields], axis=0)
    return up, down


def rows_kernel(group, b, r, c, l, agg, m, got, chip_msg, core_msg, w, mflat):
    weights(group, agg, w)
    flatten(m, mflat)
    lower = lax.axis_index("core") == 1
    left, right = side_block(got, -1), side_block(got, 1)
    up, down = row_messages(b, r, c, l, left, right)
    ww = halves(left, w, right, 4)
    half = mflat.shape[0] // 2
    mats = (left[40:], mflat[...], right[40:])
    rows = 4 * HALO
    ncol = ww.shape[1] // LANES
    for t in range(ncol):
        s = slice(t * LANES, (t + 1) * LANES)
        at = slice(rows * t, rows * (t + 1))
        core_msg[at, :] = jnp.where(lower, up[:, s], down[:, s])
        chip_msg[at, :] = jnp.where(lower, down[:, s], up[:, s])
    for t in range(0, ncol, 2):
        s, e = slice(t * LANES, (t + 1) * LANES), slice((t + 1) * LANES, (t + 2) * LANES)
        first = jnp.concatenate([ww[0:4, s], ww[0:4, e]], axis=0)
        final = jnp.concatenate([ww[4:8, s], ww[4:8, e]], axis=0)
        at = slice(rows * ncol + HALO * t, rows * ncol + HALO * (t + 2))
        core_msg[at, :] = jnp.where(lower, first, final)
        chip_msg[at, :] = jnp.where(lower, final, first)
    for i, x in enumerate(mats):
        at = slice((rows + HALO) * ncol + half * i, (rows + HALO) * ncol + half * (i + 1))
        core_msg[at, :] = jnp.where(lower, x[:half], x[half:])
        chip_msg[at, :] = jnp.where(lower, x[half:], x[:half])


def shifted(v):
    n = v.shape[1]
    r = v.shape[0]
    return (pltpu.roll(v, n - 1, 1), pltpu.roll(v, 1, 1), pltpu.roll(v, r - 1, 0), pltpu.roll(v, 1, 0))


def scaled_apply(v, east, west, south, north):
    e, w, s, n = shifted(v)
    return v - east * e - west * w - south * s - north * n


def middle(b, r, c, l, w, got, s2, s1, pre_o, z_o, east_o, west_o, south_o, north_o, msg):
    upper = lax.axis_index("core") == 0
    left, right = side_block(got, -1), side_block(got, 1)
    rows = 4 * HALO
    tiles = range(b.shape[1] // LANES + 2)
    pair, chip = [jnp.concatenate([x[rows * t : rows * (t + 1), :] for t in tiles], axis=1) for x in (s1, s2)]
    above, below = jnp.where(upper, chip, pair), jnp.where(upper, pair, chip)
    wins = []
    for i, x in enumerate((b, l, r, c)):
        at = slice(HALO * i, HALO * (i + 1))
        wins.append(jnp.concatenate([halves(left, x, right, i), below[at], above[at]], axis=0))
    bw, lw, rw, cw = wins
    n = bw.shape[1]
    ncol = n // LANES - 2
    row = lax.broadcasted_iota(jnp.int32, bw.shape, 0)
    far = jnp.logical_or(row == 11, row == 12)
    inside = jnp.logical_and(lw > 0.0, jnp.logical_not(far))
    diag, inv, coef = operator(lw, rw, cw, inside)
    z = jnp.where(far, bw, bw * inv)
    d = z * (1.0 / THETA)
    x = d
    z = jnp.where(far, lw, z - scaled_apply(d, *coef))
    d = (RHO1 * RHO0) * d + (2.0 * RHO1 / DELTA) * z
    x = x + d
    z = z - scaled_apply(d, *coef)
    d = (RHO2 * RHO1) * d + (2.0 * RHO2 / DELTA) * z
    x = x + d
    z = z - scaled_apply(d, *coef)
    own = slice(0, 8)
    g = diag[own] * (z - OMEGA * scaled_apply(z, *coef))[own]
    part = jnp.zeros((8, LANES), jnp.float32)
    for t in range(ncol):
        part = part + w[:, t * LANES : (t + 1) * LANES] * g[:, (t + 1) * LANES : (t + 2) * LANES]
    pre_o[...] = x
    z_o[...] = z
    for ref, value in zip((east_o, west_o, south_o, north_o), coef):
        ref[...] = value
    total = jnp.sum(part, axis=1, keepdims=True)
    place = (lax.axis_index("z") * 2 + lax.axis_index("core")) * 4
    lane = lax.broadcasted_iota(jnp.int32, (8, LANES), 1)
    row = lax.broadcasted_iota(jnp.int32, (8, LANES), 0)
    spread = jnp.where(lane == lax.rem(place, LANES) + row // 2, total, 0.0)
    line = jnp.sum(spread, axis=0, keepdims=True)
    rows = lax.broadcasted_iota(jnp.int32, (msg.shape[1], LANES), 0)
    msg[...] = jnp.broadcast_to(jnp.where(rows == place // LANES, line, 0.0)[None], msg.shape)


def late_kernel(w, mflat, got, s1, s2, wt, mwin):
    upper = lax.axis_index("core") == 0
    left, right = side_block(got, -1), side_block(got, 1)
    ww = halves(left, w, right, 4)
    ncol = ww.shape[1] // LANES
    pair, chip = s1[4 * HALO * ncol :, :], s2[4 * HALO * ncol :, :]
    above, below = jnp.where(upper, chip, pair), jnp.where(upper, pair, chip)
    for t in range(ncol):
        at = slice(HALO * t, HALO * (t + 1))
        s = slice(t * LANES, (t + 1) * LANES)
        wt[:, s] = jnp.concatenate([ww[:, s], below[at], above[at]], axis=0)
    half = mflat.shape[0] // 2
    for i, mine in enumerate((left[40:], mflat[...], right[40:])):
        at = slice(HALO * ncol + half * i, HALO * ncol + half * (i + 1))
        mwin[4 * half * i : 4 * half * i + half, :] = above[at]
        mwin[4 * half * i + half : 4 * half * i + 3 * half, :] = mine
        mwin[4 * half * i + 3 * half : 4 * half * (i + 1), :] = below[at]


def last(xs, gathered, mwin, pre, z_i, wt, east, west, south, north, out):
    ncols = lax.axis_size("cols")
    tiles = mwin.shape[0] // 24
    mats = [[mwin[tiles * (8 * g + k) : tiles * (8 * g + k + 1), :] for k in range(8)] for g in range(3)]
    me = lax.axis_index("cols")

    def corrections(group, mats):
        v = []
        for x in range(xs):
            v.append(gathered[(2 * x) * ncols + group] + gathered[(2 * x + 1) * ncols + group])
        v = jnp.concatenate(v, axis=0)
        lines = []
        for m in mats[2:] + mats[:2]:
            p = jnp.sum(m * v, axis=0, keepdims=True)
            lines += [p, p]
        return jnp.sum(jnp.concatenate(lines, axis=0), axis=1, keepdims=True)

    cl = corrections(jnp.maximum(me - 1, 0), mats[0])
    co = corrections(me, mats[1])
    cn = corrections(jnp.minimum(me + 1, ncols - 1), mats[2])
    w = wt[...]
    n = w.shape[1]
    lane = lax.broadcasted_iota(jnp.int32, (1, n), 1)
    lifted = w * jnp.where(lane < LANES, cl, jnp.where(lane >= n - LANES, cn, co))
    op = functools.partial(scaled_apply, east=east[...], west=west[...], south=south[...], north=north[...])
    e = lifted - OMEGA * op(lifted)
    x = pre[...] + e
    z = z_i[...] - op(e)
    d = z * (1.0 / THETA)
    x = x + d
    z = z - op(d)
    d = (RHO1 * RHO0) * d + (2.0 * RHO1 / DELTA) * z
    x = x + d
    z = z - op(d)
    d = (RHO2 * RHO1) * d + (2.0 * RHO2 / DELTA) * z
    x = x + d
    out[...] = x[0:8, LANES : n - LANES]


def local(sizes, rhs, cond_row, cond_col, leak, agg_members, coarse_inverse):
    xs, zs, cores, cols = sizes
    width = rhs.shape[1]
    wide = width + 2 * LANES
    m = coarse_inverse[0]
    tiles = m.shape[1] // LANES
    group = agg_members.shape[2] // 4
    agg = agg_members[0, 0]
    block = f32(8, width)
    edges = call(
        functools.partial(first_kernel, group),
        f32(cols, 40 + 4 * tiles, LANES),
        6,
        "first",
        space=pltpu.HBM,
        limit=FIRST_LIMIT,
        scratch=[pltpu.VMEM((8, width), jnp.float32)] * 4
        + [
            pltpu.VMEM(agg.shape, jnp.int32),
            pltpu.VMEM(m.shape, jnp.float32),
            pltpu.VMEM((8, width), jnp.float32),
            pltpu.VMEM((4 * tiles, LANES), jnp.float32),
            pltpu.SemaphoreType.DMA((10,)),
        ],
    )(rhs, cond_row, cond_col, leak, agg, m)
    b, r, c, l = rhs, cond_row, cond_col, leak
    got = lax.all_to_all(edges, "cols", 0, 0, tiled=True)
    devices = xs * zs * cores
    swap = []
    for i in range(1, devices - 1, 2):
        swap += [(i, i + 1), (i + 1, i)]
    message = f32((4 * HALO + HALO) * wide // LANES + 6 * tiles, LANES)
    chip_msg, core_msg, w, mflat = call(
        functools.partial(rows_kernel, group), [message, message, block, f32(4 * tiles, LANES)], 7, "rows"
    )(b, r, c, l, agg, m, got)
    s2 = lax.ppermute(chip_msg, ROWAX, swap)
    s1 = lax.ppermute(core_msg, "core", [(0, 1), (1, 0)])
    per_x = max(1, zs * cores * 4 // LANES)
    win = f32(WROWS, wide)
    pre, z, east, west, south, north, msg = call(middle, [win] * 6 + [f32(zs, per_x, LANES)], 8, "middle")(
        b, r, c, l, w, got, s2, s1
    )
    spread = lax.all_to_all(msg, "z", 0, 0, tiled=True)
    wt, mwin = call(late_kernel, [win, f32(24 * tiles, LANES)], 5, "late")(w, mflat, got, s1, s2)
    line = jnp.sum(spread, axis=0)
    second = jnp.broadcast_to(line[None], (xs * cores * cols, per_x, LANES))
    gathered = lax.all_to_all(second, ("x", "core", "cols"), 0, 0, tiled=True)
    return call(functools.partial(last, xs), block, 9, "last")(
        gathered, mwin, pre, z, wt, east, west, south, north
    )


def solution(mesh):
    rows, cols = mesh.shape["rows"], mesh.shape["cols"]
    cores = 2
    xs = 4 if rows == 256 else 2
    zs = rows // (xs * cores)
    fine = Mesh(mesh.devices.reshape(xs, zs, cores, cols), ("x", "z", "core", "cols"))
    spec = P(ROWAX, "cols")
    in_specs = (spec, spec, spec, spec, P(ROWAX, "cols", None, None), P("cols", ROWAX, None))
    return jax.shard_map(
        functools.partial(local, (xs, zs, cores, cols)),
        mesh=fine,
        in_specs=in_specs,
        out_specs=spec,
        check_vma=False,
    )
```

```python
import functools

import jax
import jax.numpy as jnp
from jax import lax
from jax.experimental import pallas as pl
from jax.experimental.pallas import tpu as pltpu
from jax.sharding import Mesh
from jax.sharding import PartitionSpec as P

THETA = 1.05
DELTA = 0.95
OMEGA = 2.0 / 3.0
RHO0 = DELTA / THETA
RHO1 = 1.0 / (2.0 * THETA / DELTA - RHO0)
RHO2 = 1.0 / (2.0 * THETA / DELTA - RHO1)
LANES = 128
HALO = 4
WROWS = 16
ROWAX = ("x", "z", "core")
VMEM_LIMIT = 48 * 1024 * 1024
FIRST_LIMIT = 61 * 1024 * 1024


def call(kernel, outs, nin, name, space=pltpu.VMEM, scratch=(), limit=VMEM_LIMIT):
    return pl.pallas_call(
        kernel,
        out_shape=outs,
        in_specs=[pl.BlockSpec(memory_space=space)] * nin,
        out_specs=jax.tree.map(lambda _: pl.BlockSpec(memory_space=pltpu.VMEM), outs),
        scratch_shapes=scratch,
        compiler_params=pltpu.CompilerParams(vmem_limit_bytes=limit),
        name=name,
    )


def f32(*shape):
    return jax.ShapeDtypeStruct(shape, jnp.float32)


def weights(group, agg, w_ref):
    pairs = w_ref.shape[1] // 256
    per_row = 3 * pairs
    lane = lax.broadcasted_iota(jnp.int32, (8, LANES), 1)
    row = lax.broadcasted_iota(jnp.int32, (8, LANES), 0)
    for j in range(pairs):
        base = (row * pairs + j) * 256
        p1 = agg[pl.ds(3 * j + 1, 8, stride=per_row), :]
        p2 = agg[pl.ds(3 * j + 2, 8, stride=per_row), :]
        p1 = jnp.broadcast_to(p1[:, 0:1], (8, LANES)) - base
        p2 = jnp.broadcast_to(p2[:, 0:1], (8, LANES)) - base
        s0 = 1.0 / jnp.sqrt(p1.astype(jnp.float32) * float(group))
        s1 = 1.0 / jnp.sqrt((p2 - p1).astype(jnp.float32) * float(group))
        s2 = 1.0 / jnp.sqrt((256 - p2).astype(jnp.float32) * float(group))
        for half in range(2):
            at = lane + half * LANES
            value = jnp.where(at < p1, s0, jnp.where(at < p2, s1, s2))
            w_ref[:, (2 * j + half) * LANES : (2 * j + half + 1) * LANES] = value


def flatten(m, mflat):
    tiles = m.shape[1] // LANES
    for k in range(4):
        for t in range(tiles):
            mflat[k * tiles + t : k * tiles + t + 1, :] = m[k : k + 1, t * LANES : (t + 1) * LANES]


def first_kernel(group, rhs, cr, cc, lk, agg, m, edges, b_v, r_v, c_v, l_v, agg_v, m_v, w_v, mflat, sems):
    n = w_v.shape[1]
    copies = []
    for i, (src, dst) in enumerate(((agg, agg_v), (m, m_v), (rhs, b_v), (cr, r_v), (cc, c_v), (lk, l_v))):
        for at in (slice(0, LANES), slice(n - LANES, n)):
            if i < 2:
                copy = pltpu.make_async_copy(src, dst, sems.at[len(copies)])
            else:
                copy = pltpu.make_async_copy(src.at[:, at], dst.at[:, at], sems.at[len(copies)])
            copies.append(copy)
            if i < 2:
                break
    for copy in copies:
        copy.start()
    for copy in copies:
        copy.wait()
    weights(group, agg_v, w_v)
    flatten(m_v, mflat)
    refs = (b_v, l_v, r_v, c_v, w_v)
    mine = mflat[...]
    left = jnp.concatenate([x[:, 0:LANES] for x in refs] + [mine], axis=0)
    right = jnp.concatenate([x[:, n - LANES : n] for x in refs] + [mine], axis=0)
    me = lax.axis_index("cols")
    for c in range(edges.shape[0]):
        edges[c] = jnp.where(me > c, left, right)


def side_block(got, step):
    cols = lax.axis_size("cols")
    c = lax.axis_index("cols") + step
    ok = jnp.logical_and(c >= 0, c < cols)
    return jnp.where(ok, got[jnp.clip(c, 0, cols - 1)], 0.0)


def widened(left, own, right):
    return jnp.concatenate([left, own, right], axis=1)


def halves(left, x, right, i):
    return widened(left[8 * i : 8 * i + 8], x[...], right[8 * i : 8 * i + 8])


def operator(l, r, c, inside):
    west, north = pltpu.roll(r, 1, 1), pltpu.roll(c, 1, 0)
    diag = l + r + c + west + north
    inv = jnp.where(inside, 1.0 / jnp.where(inside, diag, 1.0), 0.0)
    return diag, inv, (r * inv, west * inv, c * inv, north * inv)


def row_messages(b, r, c, l, left, right):
    bw, lw, rw, cw = [halves(left, x, right, i) for i, x in enumerate((b, l, r, c))]
    _, inv, coef = operator(lw, rw, cw, lw > 0.0)
    z0 = bw * inv
    z1 = z0 - scaled_apply(z0 * (1.0 / THETA), *coef)
    row = lax.broadcasted_iota(jnp.int32, bw.shape, 0)
    far = jnp.logical_or(row == 3, row == 4)
    fields = (jnp.where(far, z0, bw), jnp.where(far, z1, lw), rw, cw)
    up = jnp.concatenate([x[0:4] for x in fields], axis=0)
    down = jnp.concatenate([x[4:8] for x in fields], axis=0)
    return up, down


def rows_kernel(group, b, r, c, l, agg, m, got, chip_msg, core_msg, w, mflat):
    weights(group, agg, w)
    flatten(m, mflat)
    lower = lax.axis_index("core") == 1
    left, right = side_block(got, -1), side_block(got, 1)
    up, down = row_messages(b, r, c, l, left, right)
    ww = halves(left, w, right, 4)
    half = mflat.shape[0] // 2
    mats = (left[40:], mflat[...], right[40:])
    rows = 4 * HALO
    ncol = ww.shape[1] // LANES
    for t in range(ncol):
        s = slice(t * LANES, (t + 1) * LANES)
        at = slice(rows * t, rows * (t + 1))
        core_msg[at, :] = jnp.where(lower, up[:, s], down[:, s])
        chip_msg[at, :] = jnp.where(lower, down[:, s], up[:, s])
    for t in range(0, ncol, 2):
        s, e = slice(t * LANES, (t + 1) * LANES), slice((t + 1) * LANES, (t + 2) * LANES)
        first = jnp.concatenate([ww[0:4, s], ww[0:4, e]], axis=0)
        final = jnp.concatenate([ww[4:8, s], ww[4:8, e]], axis=0)
        at = slice(rows * ncol + HALO * t, rows * ncol + HALO * (t + 2))
        core_msg[at, :] = jnp.where(lower, first, final)
        chip_msg[at, :] = jnp.where(lower, final, first)
    for i, x in enumerate(mats):
        at = slice((rows + HALO) * ncol + half * i, (rows + HALO) * ncol + half * (i + 1))
        core_msg[at, :] = jnp.where(lower, x[:half], x[half:])
        chip_msg[at, :] = jnp.where(lower, x[half:], x[:half])


def shifted(v):
    n = v.shape[1]
    r = v.shape[0]
    return (pltpu.roll(v, n - 1, 1), pltpu.roll(v, 1, 1), pltpu.roll(v, r - 1, 0), pltpu.roll(v, 1, 0))


def scaled_apply(v, east, west, south, north):
    e, w, s, n = shifted(v)
    return v - east * e - west * w - south * s - north * n


def middle(b, r, c, l, w, got, s2, s1, pre_o, z_o, east_o, west_o, south_o, north_o, msg):
    upper = lax.axis_index("core") == 0
    left, right = side_block(got, -1), side_block(got, 1)
    rows = 4 * HALO
    tiles = range(b.shape[1] // LANES + 2)
    pair, chip = [jnp.concatenate([x[rows * t : rows * (t + 1), :] for t in tiles], axis=1) for x in (s1, s2)]
    above, below = jnp.where(upper, chip, pair), jnp.where(upper, pair, chip)
    wins = []
    for i, x in enumerate((b, l, r, c)):
        at = slice(HALO * i, HALO * (i + 1))
        wins.append(jnp.concatenate([halves(left, x, right, i), below[at], above[at]], axis=0))
    bw, lw, rw, cw = wins
    n = bw.shape[1]
    ncol = n // LANES - 2
    row = lax.broadcasted_iota(jnp.int32, bw.shape, 0)
    far = jnp.logical_or(row == 11, row == 12)
    inside = jnp.logical_and(lw > 0.0, jnp.logical_not(far))
    diag, inv, coef = operator(lw, rw, cw, inside)
    z = jnp.where(far, bw, bw * inv)
    d = z * (1.0 / THETA)
    x = d
    z = jnp.where(far, lw, z - scaled_apply(d, *coef))
    d = (RHO1 * RHO0) * d + (2.0 * RHO1 / DELTA) * z
    x = x + d
    z = z - scaled_apply(d, *coef)
    d = (RHO2 * RHO1) * d + (2.0 * RHO2 / DELTA) * z
    x = x + d
    z = z - scaled_apply(d, *coef)
    own = slice(0, 8)
    g = diag[own] * (z - OMEGA * scaled_apply(z, *coef))[own]
    part = jnp.zeros((8, LANES), jnp.float32)
    for t in range(ncol):
        part = part + w[:, t * LANES : (t + 1) * LANES] * g[:, (t + 1) * LANES : (t + 2) * LANES]
    pre_o[...] = x
    z_o[...] = z
    for ref, value in zip((east_o, west_o, south_o, north_o), coef):
        ref[...] = value
    total = jnp.sum(part, axis=1, keepdims=True)
    place = lax.axis_index("z") * 4
    lane = lax.broadcasted_iota(jnp.int32, (8, LANES), 1)
    row = lax.broadcasted_iota(jnp.int32, (8, LANES), 0)
    spread = jnp.where(lane == place + row // 2, total, 0.0)
    msg[...] = jnp.broadcast_to(jnp.sum(spread, axis=0, keepdims=True)[None], msg.shape)


def reordered(m):
    n = m.shape[0]
    i = lax.broadcasted_iota(jnp.int32, (LANES, LANES), 0)
    o = lax.broadcasted_iota(jnp.int32, (LANES, LANES), 1)
    source = (o % 64) // 4 * 8 + o % 4

    def pick(rows, core, high):
        chosen = jnp.logical_and(o // 64 == high, i == source + 4 * core)
        return jnp.dot(
            rows, chosen.astype(jnp.float32), precision=lax.Precision.HIGHEST, preferred_element_type=jnp.float32
        )

    even = pick(m, 0, 0) + pick(pltpu.roll(m, n - 1, 0), 0, 1)
    odd = pick(pltpu.roll(m, 1, 0), 1, 0) + pick(m, 1, 1)
    row = lax.broadcasted_iota(jnp.int32, m.shape, 0)
    return jnp.where(row % 2 == 0, even, odd)


def late_kernel(w, mflat, got, s1, s2, wt, mwin):
    upper = lax.axis_index("core") == 0
    left, right = side_block(got, -1), side_block(got, 1)
    ww = halves(left, w, right, 4)
    ncol = ww.shape[1] // LANES
    pair, chip = s1[4 * HALO * ncol :, :], s2[4 * HALO * ncol :, :]
    above, below = jnp.where(upper, chip, pair), jnp.where(upper, pair, chip)
    for t in range(ncol):
        at = slice(HALO * t, HALO * (t + 1))
        s = slice(t * LANES, (t + 1) * LANES)
        wt[:, s] = jnp.concatenate([ww[:, s], below[at], above[at]], axis=0)
    half = mflat.shape[0] // 2
    parts = []
    for i, mine in enumerate((left[40:], mflat[...], right[40:])):
        at = slice(HALO * ncol + half * i, HALO * ncol + half * (i + 1))
        parts += [above[at], mine, below[at]]
    mwin[...] = reordered(jnp.concatenate(parts, axis=0))


def last(xs, gathered, mwin, pre, z_i, wt, east, west, south, north, out):
    ncols = lax.axis_size("cols")
    tiles = mwin.shape[0] // 24
    mats = [[mwin[tiles * (8 * g + k) : tiles * (8 * g + k + 1), :] for k in range(8)] for g in range(3)]
    me = lax.axis_index("cols")

    def corrections(group, mats):
        v = jnp.concatenate([gathered[at * ncols + group] for at in range(2 * xs)], axis=0)
        lines = []
        for m in mats[2:] + mats[:2]:
            p = jnp.sum(m * v, axis=0, keepdims=True)
            lines += [p, p]
        return jnp.sum(jnp.concatenate(lines, axis=0), axis=1, keepdims=True)

    cl = corrections(jnp.maximum(me - 1, 0), mats[0])
    co = corrections(me, mats[1])
    cn = corrections(jnp.minimum(me + 1, ncols - 1), mats[2])
    w = wt[...]
    n = w.shape[1]
    lane = lax.broadcasted_iota(jnp.int32, (1, n), 1)
    lifted = w * jnp.where(lane < LANES, cl, jnp.where(lane >= n - LANES, cn, co))
    op = functools.partial(scaled_apply, east=east[...], west=west[...], south=south[...], north=north[...])
    e = lifted - OMEGA * op(lifted)
    x = pre[...] + e
    z = z_i[...] - op(e)
    d = z * (1.0 / THETA)
    x = x + d
    z = z - op(d)
    d = (RHO1 * RHO0) * d + (2.0 * RHO1 / DELTA) * z
    x = x + d
    z = z - op(d)
    d = (RHO2 * RHO1) * d + (2.0 * RHO2 / DELTA) * z
    x = x + d
    out[...] = x[0:8, LANES : n - LANES]


def local(sizes, rhs, cond_row, cond_col, leak, agg_members, coarse_inverse):
    xs, zs, cores, cols = sizes
    width = rhs.shape[1]
    wide = width + 2 * LANES
    m = coarse_inverse[0]
    tiles = m.shape[1] // LANES
    group = agg_members.shape[2] // 4
    agg = agg_members[0, 0]
    block = f32(8, width)
    edges = call(
        functools.partial(first_kernel, group),
        f32(cols, 40 + 4 * tiles, LANES),
        6,
        "first",
        space=pltpu.HBM,
        limit=FIRST_LIMIT,
        scratch=[pltpu.VMEM((8, width), jnp.float32)] * 4
        + [
            pltpu.VMEM(agg.shape, jnp.int32),
            pltpu.VMEM(m.shape, jnp.float32),
            pltpu.VMEM((8, width), jnp.float32),
            pltpu.VMEM((4 * tiles, LANES), jnp.float32),
            pltpu.SemaphoreType.DMA((10,)),
        ],
    )(rhs, cond_row, cond_col, leak, agg, m)
    b, r, c, l = rhs, cond_row, cond_col, leak
    got = lax.all_to_all(edges, "cols", 0, 0, tiled=True)
    devices = xs * zs * cores
    swap = []
    for i in range(1, devices - 1, 2):
        swap += [(i, i + 1), (i + 1, i)]
    message = f32((4 * HALO + HALO) * wide // LANES + 6 * tiles, LANES)
    chip_msg, core_msg, w, mflat = call(
        functools.partial(rows_kernel, group), [message, message, block, f32(4 * tiles, LANES)], 7, "rows"
    )(b, r, c, l, agg, m, got)
    s2 = lax.ppermute(chip_msg, ROWAX, swap)
    s1 = lax.ppermute(core_msg, "core", [(0, 1), (1, 0)])
    win = f32(WROWS, wide)
    pre, z, east, west, south, north, msg = call(middle, [win] * 6 + [f32(zs, 1, LANES)], 8, "middle")(
        b, r, c, l, w, got, s2, s1
    )
    spread = lax.all_to_all(msg, "z", 0, 0, tiled=True)
    wt, mwin = call(late_kernel, [win, f32(24 * tiles, LANES)], 5, "late")(w, mflat, got, s1, s2)
    line = jnp.sum(spread, axis=0)
    second = jnp.broadcast_to(line[None], (xs * cores * cols, 1, LANES))
    gathered = lax.all_to_all(second, ("x", "core", "cols"), 0, 0, tiled=True)
    return call(functools.partial(last, xs), block, 9, "last")(
        gathered, mwin, pre, z, wt, east, west, south, north
    )


def solution(mesh):
    rows, cols = mesh.shape["rows"], mesh.shape["cols"]
    cores = 2
    xs = 4 if rows == 256 else 2
    zs = rows // (xs * cores)
    fine = Mesh(mesh.devices.reshape(xs, zs, cores, cols), ("x", "z", "core", "cols"))
    spec = P(ROWAX, "cols")
    in_specs = (spec, spec, spec, spec, P(ROWAX, "cols", None, None), P("cols", ROWAX, None))
    return jax.shard_map(
        functools.partial(local, (xs, zs, cores, cols)),
        mesh=fine,
        in_specs=in_specs,
        out_specs=spec,
        check_vma=False,
    )
```

```python
import functools

import jax
import jax.numpy as jnp
from jax import lax
from jax.experimental import pallas as pl
from jax.experimental.pallas import tpu as pltpu
from jax.sharding import Mesh
from jax.sharding import PartitionSpec as P

THETA = 1.05
DELTA = 0.95
OMEGA = 2.0 / 3.0
RHO0 = DELTA / THETA
RHO1 = 1.0 / (2.0 * THETA / DELTA - RHO0)
RHO2 = 1.0 / (2.0 * THETA / DELTA - RHO1)
LANES = 128
HALO = 4
EDGE = 8
WROWS = 16
ROWAX = ("x", "z", "core")
VMEM_LIMIT = 48 * 1024 * 1024
FIRST_LIMIT = 61 * 1024 * 1024


def call(kernel, outs, nin, name, space=pltpu.VMEM, scratch=(), limit=VMEM_LIMIT):
    return pl.pallas_call(
        kernel,
        out_shape=outs,
        in_specs=[pl.BlockSpec(memory_space=space)] * nin,
        out_specs=jax.tree.map(lambda _: pl.BlockSpec(memory_space=pltpu.VMEM), outs),
        scratch_shapes=scratch,
        compiler_params=pltpu.CompilerParams(vmem_limit_bytes=limit),
        name=name,
    )


def f32(*shape):
    return jax.ShapeDtypeStruct(shape, jnp.float32)


def weights(group, agg, w_ref):
    pairs = w_ref.shape[1] // 256
    per_row = 3 * pairs
    lane = lax.broadcasted_iota(jnp.int32, (8, LANES), 1)
    row = lax.broadcasted_iota(jnp.int32, (8, LANES), 0)
    for j in range(pairs):
        base = (row * pairs + j) * 256
        p1 = agg[pl.ds(3 * j + 1, 8, stride=per_row), :]
        p2 = agg[pl.ds(3 * j + 2, 8, stride=per_row), :]
        p1 = jnp.broadcast_to(p1[:, 0:1], (8, LANES)) - base
        p2 = jnp.broadcast_to(p2[:, 0:1], (8, LANES)) - base
        s0 = 1.0 / jnp.sqrt(p1.astype(jnp.float32) * float(group))
        s1 = 1.0 / jnp.sqrt((p2 - p1).astype(jnp.float32) * float(group))
        s2 = 1.0 / jnp.sqrt((256 - p2).astype(jnp.float32) * float(group))
        for half in range(2):
            at = lane + half * LANES
            value = jnp.where(at < p1, s0, jnp.where(at < p2, s1, s2))
            w_ref[:, (2 * j + half) * LANES : (2 * j + half + 1) * LANES] = value


def flatten(m, mflat):
    tiles = m.shape[1] // LANES
    for k in range(4):
        for t in range(tiles):
            mflat[k * tiles + t : k * tiles + t + 1, :] = m[k : k + 1, t * LANES : (t + 1) * LANES]


def first_kernel(group, rhs, cr, cc, lk, agg, m, edges, b_v, r_v, c_v, l_v, agg_v, m_v, w_v, mflat, sems):
    n = w_v.shape[1]
    copies = []
    for i, (src, dst) in enumerate(((agg, agg_v), (m, m_v), (rhs, b_v), (cr, r_v), (cc, c_v), (lk, l_v))):
        for at in (slice(0, LANES), slice(n - LANES, n)):
            if i < 2:
                copy = pltpu.make_async_copy(src, dst, sems.at[len(copies)])
            else:
                copy = pltpu.make_async_copy(src.at[:, at], dst.at[:, at], sems.at[len(copies)])
            copies.append(copy)
            if i < 2:
                break
    for copy in copies:
        copy.start()
    for copy in copies:
        copy.wait()
    weights(group, agg_v, w_v)
    flatten(m_v, mflat)
    refs = (b_v, l_v, r_v, c_v, w_v)
    lane = lax.broadcasted_iota(jnp.int32, (8, LANES), 1)

    def packed(at, shift):
        out = jnp.zeros((8, LANES), jnp.float32)
        for i, x in enumerate(refs):
            moved = pltpu.roll(x[:, at : at + LANES], (shift + EDGE * i) % LANES, 1)
            out = jnp.where(lane // EDGE == i, moved, out)
        return jnp.concatenate([out, mflat[...]], axis=0)

    left, right = packed(0, 0), packed(n - LANES, EDGE)
    me = lax.axis_index("cols")
    for c in range(edges.shape[0]):
        edges[c] = jnp.where(me > c, left, right)


def side_block(got, step):
    cols = lax.axis_size("cols")
    c = lax.axis_index("cols") + step
    ok = jnp.logical_and(c >= 0, c < cols)
    block = jnp.where(ok, got[jnp.clip(c, 0, cols - 1)], 0.0)
    lane = lax.broadcasted_iota(jnp.int32, (8, LANES), 1)
    start = LANES - EDGE if step < 0 else 0
    near = jnp.logical_and(lane >= start, lane < start + EDGE)
    out = []
    for i in range(5):
        out.append(jnp.where(near, pltpu.roll(block[0:8], (start - EDGE * i) % LANES, 1), 0.0))
    return jnp.concatenate(out + [block[8:]], axis=0)


def widened(left, own, right):
    return jnp.concatenate([left, own, right], axis=1)


def halves(left, x, right, i):
    return widened(left[8 * i : 8 * i + 8], x[...], right[8 * i : 8 * i + 8])


def operator(l, r, c, inside):
    west, north = pltpu.roll(r, 1, 1), pltpu.roll(c, 1, 0)
    diag = l + r + c + west + north
    inv = jnp.where(inside, 1.0 / jnp.where(inside, diag, 1.0), 0.0)
    return diag, inv, (r * inv, west * inv, c * inv, north * inv)


def row_messages(b, r, c, l, left, right):
    bw, lw, rw, cw = [halves(left, x, right, i) for i, x in enumerate((b, l, r, c))]
    _, inv, coef = operator(lw, rw, cw, lw > 0.0)
    z0 = bw * inv
    z1 = z0 - scaled_apply(z0 * (1.0 / THETA), *coef)
    row = lax.broadcasted_iota(jnp.int32, bw.shape, 0)
    far = jnp.logical_or(row == 3, row == 4)
    fields = (jnp.where(far, z0, bw), jnp.where(far, z1, lw), rw, cw)
    up = jnp.concatenate([x[0:4] for x in fields], axis=0)
    down = jnp.concatenate([x[4:8] for x in fields], axis=0)
    return up, down


def rows_kernel(group, b, r, c, l, agg, m, got, chip_msg, core_msg, w, mflat):
    weights(group, agg, w)
    flatten(m, mflat)
    lower = lax.axis_index("core") == 1
    left, right = side_block(got, -1), side_block(got, 1)
    up, down = row_messages(b, r, c, l, left, right)
    ww = halves(left, w, right, 4)
    half = mflat.shape[0] // 2
    mats = (left[40:], mflat[...], right[40:])
    rows = 4 * HALO
    ncol = ww.shape[1] // LANES
    for t in range(ncol):
        s = slice(t * LANES, (t + 1) * LANES)
        at = slice(rows * t, rows * (t + 1))
        core_msg[at, :] = jnp.where(lower, up[:, s], down[:, s])
        chip_msg[at, :] = jnp.where(lower, down[:, s], up[:, s])
    for t in range(0, ncol, 2):
        s, e = slice(t * LANES, (t + 1) * LANES), slice((t + 1) * LANES, (t + 2) * LANES)
        first = jnp.concatenate([ww[0:4, s], ww[0:4, e]], axis=0)
        final = jnp.concatenate([ww[4:8, s], ww[4:8, e]], axis=0)
        at = slice(rows * ncol + HALO * t, rows * ncol + HALO * (t + 2))
        core_msg[at, :] = jnp.where(lower, first, final)
        chip_msg[at, :] = jnp.where(lower, final, first)
    for i, x in enumerate(mats):
        at = slice((rows + HALO) * ncol + half * i, (rows + HALO) * ncol + half * (i + 1))
        core_msg[at, :] = jnp.where(lower, x[:half], x[half:])
        chip_msg[at, :] = jnp.where(lower, x[half:], x[:half])


def shifted(v):
    n = v.shape[1]
    r = v.shape[0]
    return (pltpu.roll(v, n - 1, 1), pltpu.roll(v, 1, 1), pltpu.roll(v, r - 1, 0), pltpu.roll(v, 1, 0))


def scaled_apply(v, east, west, south, north):
    e, w, s, n = shifted(v)
    return v - east * e - west * w - south * s - north * n


def middle(b, r, c, l, w, got, s2, s1, pre_o, z_o, east_o, west_o, south_o, north_o, msg):
    upper = lax.axis_index("core") == 0
    left, right = side_block(got, -1), side_block(got, 1)
    rows = 4 * HALO
    tiles = range(b.shape[1] // LANES + 2)
    pair, chip = [jnp.concatenate([x[rows * t : rows * (t + 1), :] for t in tiles], axis=1) for x in (s1, s2)]
    above, below = jnp.where(upper, chip, pair), jnp.where(upper, pair, chip)
    wins = []
    for i, x in enumerate((b, l, r, c)):
        at = slice(HALO * i, HALO * (i + 1))
        wins.append(jnp.concatenate([halves(left, x, right, i), below[at], above[at]], axis=0))
    bw, lw, rw, cw = wins
    n = bw.shape[1]
    ncol = n // LANES - 2
    row = lax.broadcasted_iota(jnp.int32, bw.shape, 0)
    far = jnp.logical_or(row == 11, row == 12)
    inside = jnp.logical_and(lw > 0.0, jnp.logical_not(far))
    diag, inv, coef = operator(lw, rw, cw, inside)
    z = jnp.where(far, bw, bw * inv)
    d = z * (1.0 / THETA)
    x = d
    z = jnp.where(far, lw, z - scaled_apply(d, *coef))
    d = (RHO1 * RHO0) * d + (2.0 * RHO1 / DELTA) * z
    x = x + d
    z = z - scaled_apply(d, *coef)
    d = (RHO2 * RHO1) * d + (2.0 * RHO2 / DELTA) * z
    x = x + d
    z = z - scaled_apply(d, *coef)
    own = slice(0, 8)
    g = diag[own] * (z - OMEGA * scaled_apply(z, *coef))[own]
    part = jnp.zeros((8, LANES), jnp.float32)
    for t in range(ncol):
        part = part + w[:, t * LANES : (t + 1) * LANES] * g[:, (t + 1) * LANES : (t + 2) * LANES]
    pre_o[...] = x
    z_o[...] = z
    for ref, value in zip((east_o, west_o, south_o, north_o), coef):
        ref[...] = value
    total = jnp.sum(part, axis=1, keepdims=True)
    place = lax.axis_index("z") * 4
    lane = lax.broadcasted_iota(jnp.int32, (8, LANES), 1)
    row = lax.broadcasted_iota(jnp.int32, (8, LANES), 0)
    spread = jnp.where(lane == place + row // 2, total, 0.0)
    msg[...] = jnp.broadcast_to(jnp.sum(spread, axis=0, keepdims=True)[None], msg.shape)


def reordered(m):
    n = m.shape[0]
    i = lax.broadcasted_iota(jnp.int32, (LANES, LANES), 0)
    o = lax.broadcasted_iota(jnp.int32, (LANES, LANES), 1)
    source = (o % 64) // 4 * 8 + o % 4

    def pick(rows, core, high):
        chosen = jnp.logical_and(o // 64 == high, i == source + 4 * core)
        return jnp.dot(
            rows, chosen.astype(jnp.float32), precision=lax.Precision.HIGHEST, preferred_element_type=jnp.float32
        )

    even = pick(m, 0, 0) + pick(pltpu.roll(m, n - 1, 0), 0, 1)
    odd = pick(pltpu.roll(m, 1, 0), 1, 0) + pick(m, 1, 1)
    row = lax.broadcasted_iota(jnp.int32, m.shape, 0)
    return jnp.where(row % 2 == 0, even, odd)


def late_kernel(w, mflat, got, s1, s2, wt, mwin):
    upper = lax.axis_index("core") == 0
    left, right = side_block(got, -1), side_block(got, 1)
    ww = halves(left, w, right, 4)
    ncol = ww.shape[1] // LANES
    pair, chip = s1[4 * HALO * ncol :, :], s2[4 * HALO * ncol :, :]
    above, below = jnp.where(upper, chip, pair), jnp.where(upper, pair, chip)
    for t in range(ncol):
        at = slice(HALO * t, HALO * (t + 1))
        s = slice(t * LANES, (t + 1) * LANES)
        wt[:, s] = jnp.concatenate([ww[:, s], below[at], above[at]], axis=0)
    half = mflat.shape[0] // 2
    parts = []
    for i, mine in enumerate((left[40:], mflat[...], right[40:])):
        at = slice(HALO * ncol + half * i, HALO * ncol + half * (i + 1))
        parts += [above[at], mine, below[at]]
    mwin[...] = reordered(jnp.concatenate(parts, axis=0))


def last(xs, gathered, mwin, pre, z_i, wt, east, west, south, north, out):
    ncols = lax.axis_size("cols")
    tiles = mwin.shape[0] // 24
    mats = [[mwin[tiles * (8 * g + k) : tiles * (8 * g + k + 1), :] for k in range(8)] for g in range(3)]
    me = lax.axis_index("cols")

    def corrections(group, mats):
        v = jnp.concatenate([gathered[at * ncols + group] for at in range(2 * xs)], axis=0)
        lines = []
        for m in mats[2:] + mats[:2]:
            p = jnp.sum(m * v, axis=0, keepdims=True)
            lines += [p, p]
        return jnp.sum(jnp.concatenate(lines, axis=0), axis=1, keepdims=True)

    cl = corrections(jnp.maximum(me - 1, 0), mats[0])
    co = corrections(me, mats[1])
    cn = corrections(jnp.minimum(me + 1, ncols - 1), mats[2])
    w = wt[...]
    n = w.shape[1]
    lane = lax.broadcasted_iota(jnp.int32, (1, n), 1)
    lifted = w * jnp.where(lane < LANES, cl, jnp.where(lane >= n - LANES, cn, co))
    op = functools.partial(scaled_apply, east=east[...], west=west[...], south=south[...], north=north[...])
    e = lifted - OMEGA * op(lifted)
    x = pre[...] + e
    z = z_i[...] - op(e)
    d = z * (1.0 / THETA)
    x = x + d
    z = z - op(d)
    d = (RHO1 * RHO0) * d + (2.0 * RHO1 / DELTA) * z
    x = x + d
    z = z - op(d)
    d = (RHO2 * RHO1) * d + (2.0 * RHO2 / DELTA) * z
    x = x + d
    out[...] = x[0:8, LANES : n - LANES]


def local(sizes, rhs, cond_row, cond_col, leak, agg_members, coarse_inverse):
    xs, zs, cores, cols = sizes
    width = rhs.shape[1]
    wide = width + 2 * LANES
    m = coarse_inverse[0]
    tiles = m.shape[1] // LANES
    group = agg_members.shape[2] // 4
    agg = agg_members[0, 0]
    block = f32(8, width)
    edges = call(
        functools.partial(first_kernel, group),
        f32(cols, 8 + 4 * tiles, LANES),
        6,
        "first",
        space=pltpu.HBM,
        limit=FIRST_LIMIT,
        scratch=[pltpu.VMEM((8, width), jnp.float32)] * 4
        + [
            pltpu.VMEM(agg.shape, jnp.int32),
            pltpu.VMEM(m.shape, jnp.float32),
            pltpu.VMEM((8, width), jnp.float32),
            pltpu.VMEM((4 * tiles, LANES), jnp.float32),
            pltpu.SemaphoreType.DMA((10,)),
        ],
    )(rhs, cond_row, cond_col, leak, agg, m)
    b, r, c, l = rhs, cond_row, cond_col, leak
    got = lax.all_to_all(edges, "cols", 0, 0, tiled=True)
    devices = xs * zs * cores
    swap = []
    for i in range(1, devices - 1, 2):
        swap += [(i, i + 1), (i + 1, i)]
    message = f32((4 * HALO + HALO) * wide // LANES + 6 * tiles, LANES)
    chip_msg, core_msg, w, mflat = call(
        functools.partial(rows_kernel, group), [message, message, block, f32(4 * tiles, LANES)], 7, "rows"
    )(b, r, c, l, agg, m, got)
    s2 = lax.ppermute(chip_msg, ROWAX, swap)
    s1 = lax.ppermute(core_msg, "core", [(0, 1), (1, 0)])
    win = f32(WROWS, wide)
    pre, z, east, west, south, north, msg = call(middle, [win] * 6 + [f32(zs, 1, LANES)], 8, "middle")(
        b, r, c, l, w, got, s2, s1
    )
    spread = lax.all_to_all(msg, "z", 0, 0, tiled=True)
    wt, mwin = call(late_kernel, [win, f32(24 * tiles, LANES)], 5, "late")(w, mflat, got, s1, s2)
    line = jnp.sum(spread, axis=0)
    second = jnp.broadcast_to(line[None], (xs * cores * cols, 1, LANES))
    gathered = lax.all_to_all(second, ("x", "core", "cols"), 0, 0, tiled=True)
    return call(functools.partial(last, xs), block, 9, "last")(
        gathered, mwin, pre, z, wt, east, west, south, north
    )


def solution(mesh):
    rows, cols = mesh.shape["rows"], mesh.shape["cols"]
    cores = 2
    xs = 4 if rows == 256 else 2
    zs = rows // (xs * cores)
    fine = Mesh(mesh.devices.reshape(xs, zs, cores, cols), ("x", "z", "core", "cols"))
    spec = P(ROWAX, "cols")
    in_specs = (spec, spec, spec, spec, P(ROWAX, "cols", None, None), P("cols", ROWAX, None))
    return jax.shard_map(
        functools.partial(local, (xs, zs, cores, cols)),
        mesh=fine,
        in_specs=in_specs,
        out_specs=spec,
        check_vma=False,
    )
```

```python
import functools

import jax
import jax.numpy as jnp
from jax import lax
from jax.experimental import pallas as pl
from jax.experimental.pallas import tpu as pltpu
from jax.sharding import Mesh
from jax.sharding import PartitionSpec as P

THETA = 1.05
DELTA = 0.95
OMEGA = 2.0 / 3.0
RHO0 = DELTA / THETA
RHO1 = 1.0 / (2.0 * THETA / DELTA - RHO0)
RHO2 = 1.0 / (2.0 * THETA / DELTA - RHO1)
LANES = 128
HALO = 4
EDGE = 8
WROWS = 16
ROWAX = ("x", "z", "core")
VMEM_LIMIT = 48 * 1024 * 1024
FIRST_LIMIT = 61 * 1024 * 1024


def call(kernel, outs, nin, name, space=pltpu.VMEM, scratch=(), limit=VMEM_LIMIT):
    return pl.pallas_call(
        kernel,
        out_shape=outs,
        in_specs=[pl.BlockSpec(memory_space=space)] * nin,
        out_specs=jax.tree.map(lambda _: pl.BlockSpec(memory_space=pltpu.VMEM), outs),
        scratch_shapes=scratch,
        compiler_params=pltpu.CompilerParams(vmem_limit_bytes=limit),
        name=name,
    )


def f32(*shape):
    return jax.ShapeDtypeStruct(shape, jnp.float32)


def weights(group, agg, w_ref):
    pairs = w_ref.shape[1] // 256
    per_row = 3 * pairs
    lane = lax.broadcasted_iota(jnp.int32, (8, LANES), 1)
    row = lax.broadcasted_iota(jnp.int32, (8, LANES), 0)
    for j in range(pairs):
        base = (row * pairs + j) * 256
        p1 = agg[pl.ds(3 * j + 1, 8, stride=per_row), :]
        p2 = agg[pl.ds(3 * j + 2, 8, stride=per_row), :]
        p1 = jnp.broadcast_to(p1[:, 0:1], (8, LANES)) - base
        p2 = jnp.broadcast_to(p2[:, 0:1], (8, LANES)) - base
        s0 = 1.0 / jnp.sqrt(p1.astype(jnp.float32) * float(group))
        s1 = 1.0 / jnp.sqrt((p2 - p1).astype(jnp.float32) * float(group))
        s2 = 1.0 / jnp.sqrt((256 - p2).astype(jnp.float32) * float(group))
        for half in range(2):
            at = lane + half * LANES
            value = jnp.where(at < p1, s0, jnp.where(at < p2, s1, s2))
            w_ref[:, (2 * j + half) * LANES : (2 * j + half + 1) * LANES] = value


def flatten(m, mflat):
    tiles = m.shape[1] // LANES
    for k in range(4):
        for t in range(tiles):
            mflat[k * tiles + t : k * tiles + t + 1, :] = m[k : k + 1, t * LANES : (t + 1) * LANES]
    mflat[...] = reordered(mflat[...])


def first_kernel(group, rhs, cr, cc, lk, agg, m, edges, b_v, r_v, c_v, l_v, agg_v, m_v, w_v, mflat, sems):
    n = w_v.shape[1]
    copies = []
    for i, (src, dst) in enumerate(((agg, agg_v), (m, m_v), (rhs, b_v), (cr, r_v), (cc, c_v), (lk, l_v))):
        for at in (slice(0, LANES), slice(n - LANES, n)):
            if i < 2:
                copy = pltpu.make_async_copy(src, dst, sems.at[len(copies)])
            else:
                copy = pltpu.make_async_copy(src.at[:, at], dst.at[:, at], sems.at[len(copies)])
            copies.append(copy)
            if i < 2:
                break
    for copy in copies:
        copy.start()
    for copy in copies:
        copy.wait()
    weights(group, agg_v, w_v)
    flatten(m_v, mflat)
    refs = (b_v, l_v, r_v, c_v, w_v)
    lane = lax.broadcasted_iota(jnp.int32, (8, LANES), 1)

    def packed(at, shift):
        out = jnp.zeros((8, LANES), jnp.float32)
        for i, x in enumerate(refs):
            moved = pltpu.roll(x[:, at : at + LANES], (shift + EDGE * i) % LANES, 1)
            out = jnp.where(lane // EDGE == i, moved, out)
        return jnp.concatenate([out, mflat[...]], axis=0)

    left, right = packed(0, 0), packed(n - LANES, EDGE)
    me = lax.axis_index("cols")
    for c in range(edges.shape[0]):
        edges[c] = jnp.where(me > c, left, right)


def side_block(got, step):
    cols = lax.axis_size("cols")
    c = lax.axis_index("cols") + step
    ok = jnp.logical_and(c >= 0, c < cols)
    block = jnp.where(ok, got[jnp.clip(c, 0, cols - 1)], 0.0)
    lane = lax.broadcasted_iota(jnp.int32, (8, LANES), 1)
    start = LANES - EDGE if step < 0 else 0
    near = jnp.logical_and(lane >= start, lane < start + EDGE)
    out = []
    for i in range(5):
        out.append(jnp.where(near, pltpu.roll(block[0:8], (start - EDGE * i) % LANES, 1), 0.0))
    return jnp.concatenate(out + [block[8:]], axis=0)


def widened(left, own, right):
    return jnp.concatenate([left, own, right], axis=1)


def halves(left, x, right, i):
    return widened(left[8 * i : 8 * i + 8], x[...], right[8 * i : 8 * i + 8])


def operator(l, r, c, inside):
    west, north = pltpu.roll(r, 1, 1), pltpu.roll(c, 1, 0)
    diag = l + r + c + west + north
    inv = jnp.where(inside, 1.0 / jnp.where(inside, diag, 1.0), 0.0)
    return diag, inv, (r * inv, west * inv, c * inv, north * inv)


def row_messages(b, r, c, l, left, right):
    bw, lw, rw, cw = [halves(left, x, right, i) for i, x in enumerate((b, l, r, c))]
    _, inv, coef = operator(lw, rw, cw, lw > 0.0)
    z0 = bw * inv
    z1 = z0 - scaled_apply(z0 * (1.0 / THETA), *coef)
    row = lax.broadcasted_iota(jnp.int32, bw.shape, 0)
    far = jnp.logical_or(row == 3, row == 4)
    fields = (jnp.where(far, z0, bw), jnp.where(far, z1, lw), rw, cw)
    up = jnp.concatenate([x[0:4] for x in fields], axis=0)
    down = jnp.concatenate([x[4:8] for x in fields], axis=0)
    return up, down


def rows_kernel(group, b, r, c, l, agg, m, got, chip_msg, core_msg, w, mflat):
    weights(group, agg, w)
    flatten(m, mflat)
    lower = lax.axis_index("core") == 1
    left, right = side_block(got, -1), side_block(got, 1)
    up, down = row_messages(b, r, c, l, left, right)
    ww = halves(left, w, right, 4)
    half = mflat.shape[0] // 2
    mats = (left[40:], mflat[...], right[40:])
    rows = 4 * HALO
    ncol = ww.shape[1] // LANES
    for t in range(ncol):
        s = slice(t * LANES, (t + 1) * LANES)
        at = slice(rows * t, rows * (t + 1))
        core_msg[at, :] = jnp.where(lower, up[:, s], down[:, s])
        chip_msg[at, :] = jnp.where(lower, down[:, s], up[:, s])
    for t in range(0, ncol, 2):
        s, e = slice(t * LANES, (t + 1) * LANES), slice((t + 1) * LANES, (t + 2) * LANES)
        first = jnp.concatenate([ww[0:4, s], ww[0:4, e]], axis=0)
        final = jnp.concatenate([ww[4:8, s], ww[4:8, e]], axis=0)
        at = slice(rows * ncol + HALO * t, rows * ncol + HALO * (t + 2))
        core_msg[at, :] = jnp.where(lower, first, final)
        chip_msg[at, :] = jnp.where(lower, final, first)
    for i, x in enumerate(mats):
        at = slice((rows + HALO) * ncol + half * i, (rows + HALO) * ncol + half * (i + 1))
        core_msg[at, :] = jnp.where(lower, x[:half], x[half:])
        chip_msg[at, :] = jnp.where(lower, x[half:], x[:half])


def shifted(v):
    n = v.shape[1]
    r = v.shape[0]
    return (pltpu.roll(v, n - 1, 1), pltpu.roll(v, 1, 1), pltpu.roll(v, r - 1, 0), pltpu.roll(v, 1, 0))


def scaled_apply(v, east, west, south, north):
    e, w, s, n = shifted(v)
    return v - east * e - west * w - south * s - north * n


def middle(b, r, c, l, w, mflat, got, s2, s1, pre_o, z_o, east_o, west_o, south_o, north_o, wt, mwin, msg):
    late_windows(w, mflat, got, s1, s2, wt, mwin)
    upper = lax.axis_index("core") == 0
    left, right = side_block(got, -1), side_block(got, 1)
    rows = 4 * HALO
    tiles = range(b.shape[1] // LANES + 2)
    pair, chip = [jnp.concatenate([x[rows * t : rows * (t + 1), :] for t in tiles], axis=1) for x in (s1, s2)]
    above, below = jnp.where(upper, chip, pair), jnp.where(upper, pair, chip)
    wins = []
    for i, x in enumerate((b, l, r, c)):
        at = slice(HALO * i, HALO * (i + 1))
        wins.append(jnp.concatenate([halves(left, x, right, i), below[at], above[at]], axis=0))
    bw, lw, rw, cw = wins
    n = bw.shape[1]
    ncol = n // LANES - 2
    row = lax.broadcasted_iota(jnp.int32, bw.shape, 0)
    far = jnp.logical_or(row == 11, row == 12)
    inside = jnp.logical_and(lw > 0.0, jnp.logical_not(far))
    diag, inv, coef = operator(lw, rw, cw, inside)
    z = jnp.where(far, bw, bw * inv)
    d = z * (1.0 / THETA)
    x = d
    z = jnp.where(far, lw, z - scaled_apply(d, *coef))
    d = (RHO1 * RHO0) * d + (2.0 * RHO1 / DELTA) * z
    x = x + d
    z = z - scaled_apply(d, *coef)
    d = (RHO2 * RHO1) * d + (2.0 * RHO2 / DELTA) * z
    x = x + d
    z = z - scaled_apply(d, *coef)
    own = slice(0, 8)
    g = diag[own] * (z - OMEGA * scaled_apply(z, *coef))[own]
    part = jnp.zeros((8, LANES), jnp.float32)
    for t in range(ncol):
        part = part + w[:, t * LANES : (t + 1) * LANES] * g[:, (t + 1) * LANES : (t + 2) * LANES]
    pre_o[...] = x
    z_o[...] = z
    for ref, value in zip((east_o, west_o, south_o, north_o), coef):
        ref[...] = value
    total = jnp.sum(part, axis=1, keepdims=True)
    place = lax.axis_index("z") * 4
    lane = lax.broadcasted_iota(jnp.int32, (8, LANES), 1)
    row = lax.broadcasted_iota(jnp.int32, (8, LANES), 0)
    spread = jnp.where(lane == place + row // 2, total, 0.0)
    msg[...] = jnp.broadcast_to(jnp.sum(spread, axis=0, keepdims=True)[None], msg.shape)


def reordered(m):
    n = m.shape[0]
    i = lax.broadcasted_iota(jnp.int32, (LANES, LANES), 0)
    o = lax.broadcasted_iota(jnp.int32, (LANES, LANES), 1)
    source = (o % 64) // 4 * 8 + o % 4

    def pick(rows, core, high):
        chosen = jnp.logical_and(o // 64 == high, i == source + 4 * core)
        return jnp.dot(
            rows, chosen.astype(jnp.float32), precision=lax.Precision.HIGHEST, preferred_element_type=jnp.float32
        )

    even = pick(m, 0, 0) + pick(pltpu.roll(m, n - 1, 0), 0, 1)
    odd = pick(pltpu.roll(m, 1, 0), 1, 0) + pick(m, 1, 1)
    row = lax.broadcasted_iota(jnp.int32, m.shape, 0)
    return jnp.where(row % 2 == 0, even, odd)


def late_windows(w, mflat, got, s1, s2, wt, mwin):
    upper = lax.axis_index("core") == 0
    left, right = side_block(got, -1), side_block(got, 1)
    ww = halves(left, w, right, 4)
    ncol = ww.shape[1] // LANES
    pair, chip = s1[4 * HALO * ncol :, :], s2[4 * HALO * ncol :, :]
    above, below = jnp.where(upper, chip, pair), jnp.where(upper, pair, chip)
    for t in range(ncol):
        at = slice(HALO * t, HALO * (t + 1))
        s = slice(t * LANES, (t + 1) * LANES)
        wt[:, s] = jnp.concatenate([ww[:, s], below[at], above[at]], axis=0)
    half = mflat.shape[0] // 2
    parts = []
    for i, mine in enumerate((left[40:], mflat[...], right[40:])):
        at = slice(HALO * ncol + half * i, HALO * ncol + half * (i + 1))
        parts += [above[at], mine, below[at]]
    mwin[...] = jnp.concatenate(parts, axis=0)


def last(xs, gathered, mwin, pre, z_i, wt, east, west, south, north, out):
    ncols = lax.axis_size("cols")
    tiles = mwin.shape[0] // 24
    mats = [[mwin[tiles * (8 * g + k) : tiles * (8 * g + k + 1), :] for k in range(8)] for g in range(3)]
    me = lax.axis_index("cols")

    def corrections(group, mats):
        v = jnp.concatenate([gathered[at * ncols + group] for at in range(2 * xs)], axis=0)
        lines = []
        for m in mats[2:] + mats[:2]:
            p = jnp.sum(m * v, axis=0, keepdims=True)
            lines += [p, p]
        return jnp.sum(jnp.concatenate(lines, axis=0), axis=1, keepdims=True)

    cl = corrections(jnp.maximum(me - 1, 0), mats[0])
    co = corrections(me, mats[1])
    cn = corrections(jnp.minimum(me + 1, ncols - 1), mats[2])
    w = wt[...]
    n = w.shape[1]
    lane = lax.broadcasted_iota(jnp.int32, (1, n), 1)
    lifted = w * jnp.where(lane < LANES, cl, jnp.where(lane >= n - LANES, cn, co))
    op = functools.partial(scaled_apply, east=east[...], west=west[...], south=south[...], north=north[...])
    e = lifted - OMEGA * op(lifted)
    x = pre[...] + e
    z = z_i[...] - op(e)
    d = z * (1.0 / THETA)
    x = x + d
    z = z - op(d)
    d = (RHO1 * RHO0) * d + (2.0 * RHO1 / DELTA) * z
    x = x + d
    z = z - op(d)
    d = (RHO2 * RHO1) * d + (2.0 * RHO2 / DELTA) * z
    x = x + d
    out[...] = x[0:8, LANES : n - LANES]


def local(sizes, rhs, cond_row, cond_col, leak, agg_members, coarse_inverse):
    xs, zs, cores, cols = sizes
    width = rhs.shape[1]
    wide = width + 2 * LANES
    m = coarse_inverse[0]
    tiles = m.shape[1] // LANES
    group = agg_members.shape[2] // 4
    agg = agg_members[0, 0]
    block = f32(8, width)
    edges = call(
        functools.partial(first_kernel, group),
        f32(cols, 8 + 4 * tiles, LANES),
        6,
        "first",
        space=pltpu.HBM,
        limit=FIRST_LIMIT,
        scratch=[pltpu.VMEM((8, width), jnp.float32)] * 4
        + [
            pltpu.VMEM(agg.shape, jnp.int32),
            pltpu.VMEM(m.shape, jnp.float32),
            pltpu.VMEM((8, width), jnp.float32),
            pltpu.VMEM((4 * tiles, LANES), jnp.float32),
            pltpu.SemaphoreType.DMA((10,)),
        ],
    )(rhs, cond_row, cond_col, leak, agg, m)
    b, r, c, l = rhs, cond_row, cond_col, leak
    got = lax.all_to_all(edges, "cols", 0, 0, tiled=True)
    devices = xs * zs * cores
    swap = []
    for i in range(1, devices - 1, 2):
        swap += [(i, i + 1), (i + 1, i)]
    message = f32((4 * HALO + HALO) * wide // LANES + 6 * tiles, LANES)
    chip_msg, core_msg, w, mflat = call(
        functools.partial(rows_kernel, group), [message, message, block, f32(4 * tiles, LANES)], 7, "rows"
    )(b, r, c, l, agg, m, got)
    s2 = lax.ppermute(chip_msg, ROWAX, swap)
    s1 = lax.ppermute(core_msg, "core", [(0, 1), (1, 0)])
    win = f32(WROWS, wide)
    pre, z, east, west, south, north, wt, mwin, msg = call(
        middle, [win] * 7 + [f32(24 * tiles, LANES), f32(zs, 1, LANES)], 9, "middle"
    )(b, r, c, l, w, mflat, got, s2, s1)
    spread = lax.all_to_all(msg, "z", 0, 0, tiled=True)
    line = jnp.sum(spread, axis=0)
    second = jnp.broadcast_to(line[None], (xs * cores * cols, 1, LANES))
    gathered = lax.all_to_all(second, ("x", "core", "cols"), 0, 0, tiled=True)
    return call(functools.partial(last, xs), block, 9, "last")(
        gathered, mwin, pre, z, wt, east, west, south, north
    )


def solution(mesh):
    rows, cols = mesh.shape["rows"], mesh.shape["cols"]
    cores = 2
    xs = 4 if rows == 256 else 2
    zs = rows // (xs * cores)
    fine = Mesh(mesh.devices.reshape(xs, zs, cores, cols), ("x", "z", "core", "cols"))
    spec = P(ROWAX, "cols")
    in_specs = (spec, spec, spec, spec, P(ROWAX, "cols", None, None), P("cols", ROWAX, None))
    return jax.shard_map(
        functools.partial(local, (xs, zs, cores, cols)),
        mesh=fine,
        in_specs=in_specs,
        out_specs=spec,
        check_vma=False,
    )
```

```python
import functools

import jax
import jax.numpy as jnp
from jax import lax
from jax.experimental import pallas as pl
from jax.experimental.pallas import tpu as pltpu
from jax.sharding import Mesh
from jax.sharding import PartitionSpec as P

THETA = 1.05
DELTA = 0.95
OMEGA = 2.0 / 3.0
RHO0 = DELTA / THETA
RHO1 = 1.0 / (2.0 * THETA / DELTA - RHO0)
RHO2 = 1.0 / (2.0 * THETA / DELTA - RHO1)
LANES = 128
HALO = 4
EDGE = 8
WROWS = 16
ROWAX = ("x", "z", "core")
VMEM_LIMIT = 48 * 1024 * 1024
FIRST_LIMIT = 61 * 1024 * 1024


def call(kernel, outs, nin, name, space=pltpu.VMEM, scratch=(), limit=VMEM_LIMIT):
    return pl.pallas_call(
        kernel,
        out_shape=outs,
        in_specs=[pl.BlockSpec(memory_space=space)] * nin,
        out_specs=jax.tree.map(lambda _: pl.BlockSpec(memory_space=pltpu.VMEM), outs),
        scratch_shapes=scratch,
        compiler_params=pltpu.CompilerParams(vmem_limit_bytes=limit),
        name=name,
    )


def f32(*shape):
    return jax.ShapeDtypeStruct(shape, jnp.float32)


def weights(group, agg, w_ref):
    pairs = w_ref.shape[1] // 256
    per_row = 3 * pairs
    lane = lax.broadcasted_iota(jnp.int32, (8, LANES), 1)
    row = lax.broadcasted_iota(jnp.int32, (8, LANES), 0)
    for j in range(pairs):
        base = (row * pairs + j) * 256
        p1 = agg[pl.ds(3 * j + 1, 8, stride=per_row), :]
        p2 = agg[pl.ds(3 * j + 2, 8, stride=per_row), :]
        p1 = jnp.broadcast_to(p1[:, 0:1], (8, LANES)) - base
        p2 = jnp.broadcast_to(p2[:, 0:1], (8, LANES)) - base
        s0 = 1.0 / jnp.sqrt(p1.astype(jnp.float32) * float(group))
        s1 = 1.0 / jnp.sqrt((p2 - p1).astype(jnp.float32) * float(group))
        s2 = 1.0 / jnp.sqrt((256 - p2).astype(jnp.float32) * float(group))
        for half in range(2):
            at = lane + half * LANES
            value = jnp.where(at < p1, s0, jnp.where(at < p2, s1, s2))
            w_ref[:, (2 * j + half) * LANES : (2 * j + half + 1) * LANES] = value


def flatten(m, mflat):
    tiles = m.shape[1] // LANES
    for k in range(4):
        for t in range(tiles):
            mflat[k * tiles + t : k * tiles + t + 1, :] = m[k : k + 1, t * LANES : (t + 1) * LANES]
    mflat[...] = reordered(mflat[...])


def first_kernel(group, rhs, cr, cc, lk, agg, m, edges, b_v, r_v, c_v, l_v, agg_v, m_v, w_v, mflat, sems):
    n = w_v.shape[1]
    copies = []
    for i, (src, dst) in enumerate(((agg, agg_v), (m, m_v), (rhs, b_v), (cr, r_v), (cc, c_v), (lk, l_v))):
        for at in (slice(0, LANES), slice(n - LANES, n)):
            if i < 2:
                copy = pltpu.make_async_copy(src, dst, sems.at[len(copies)])
            else:
                copy = pltpu.make_async_copy(src.at[:, at], dst.at[:, at], sems.at[len(copies)])
            copies.append(copy)
            if i < 2:
                break
    for copy in copies:
        copy.start()
    for copy in copies:
        copy.wait()
    weights(group, agg_v, w_v)
    flatten(m_v, mflat)
    refs = (b_v, l_v, r_v, c_v, w_v)
    lane = lax.broadcasted_iota(jnp.int32, (8, LANES), 1)

    def packed(at, shift):
        out = jnp.zeros((8, LANES), jnp.float32)
        for i, x in enumerate(refs):
            moved = pltpu.roll(x[:, at : at + LANES], (shift + EDGE * i) % LANES, 1)
            out = jnp.where(lane // EDGE == i, moved, out)
        return jnp.concatenate([out, mflat[...]], axis=0)

    left, right = packed(0, 0), packed(n - LANES, EDGE)
    me = lax.axis_index("cols")
    for c in range(edges.shape[0]):
        edges[c] = jnp.where(me > c, left, right)


def side_block(got, step):
    cols = lax.axis_size("cols")
    c = lax.axis_index("cols") + step
    ok = jnp.logical_and(c >= 0, c < cols)
    block = jnp.where(ok, got[jnp.clip(c, 0, cols - 1)], 0.0)
    lane = lax.broadcasted_iota(jnp.int32, (8, LANES), 1)
    start = LANES - EDGE if step < 0 else 0
    near = jnp.logical_and(lane >= start, lane < start + EDGE)
    out = []
    for i in range(5):
        out.append(jnp.where(near, pltpu.roll(block[0:8], (start - EDGE * i) % LANES, 1), 0.0))
    return jnp.concatenate(out + [block[8:]], axis=0)


def widened(left, own, right):
    return jnp.concatenate([left, own, right], axis=1)


def halves(left, x, right, i):
    return widened(left[8 * i : 8 * i + 8], x[...], right[8 * i : 8 * i + 8])


def operator(l, r, c, inside):
    west, north = pltpu.roll(r, 1, 1), pltpu.roll(c, 1, 0)
    diag = l + r + c + west + north
    inv = jnp.where(inside, 1.0 / jnp.where(inside, diag, 1.0), 0.0)
    return diag, inv, (r * inv, west * inv, c * inv, north * inv)


def row_messages(b, r, c, l, left, right):
    bw, lw, rw, cw = [halves(left, x, right, i) for i, x in enumerate((b, l, r, c))]
    _, inv, coef = operator(lw, rw, cw, lw > 0.0)
    z0 = bw * inv
    z1 = z0 - scaled_apply(z0 * (1.0 / THETA), *coef)
    row = lax.broadcasted_iota(jnp.int32, bw.shape, 0)
    far = jnp.logical_or(row == 3, row == 4)
    fields = (jnp.where(far, z0, bw), jnp.where(far, z1, lw), rw, cw)
    up = jnp.concatenate([x[0:4] for x in fields], axis=0)
    down = jnp.concatenate([x[4:8] for x in fields], axis=0)
    return up, down


def rows_kernel(group, b, r, c, l, agg, got, chip_msg, core_msg, w, mflat):
    weights(group, agg, w)
    mflat[...] = got[lax.axis_index("cols")][8:]
    lower = lax.axis_index("core") == 1
    left, right = side_block(got, -1), side_block(got, 1)
    up, down = row_messages(b, r, c, l, left, right)
    ww = halves(left, w, right, 4)
    half = mflat.shape[0] // 2
    mats = (left[40:], mflat[...], right[40:])
    rows = 4 * HALO
    ncol = ww.shape[1] // LANES
    for t in range(ncol):
        s = slice(t * LANES, (t + 1) * LANES)
        at = slice(rows * t, rows * (t + 1))
        core_msg[at, :] = jnp.where(lower, up[:, s], down[:, s])
        chip_msg[at, :] = jnp.where(lower, down[:, s], up[:, s])
    for t in range(0, ncol, 2):
        s, e = slice(t * LANES, (t + 1) * LANES), slice((t + 1) * LANES, (t + 2) * LANES)
        first = jnp.concatenate([ww[0:4, s], ww[0:4, e]], axis=0)
        final = jnp.concatenate([ww[4:8, s], ww[4:8, e]], axis=0)
        at = slice(rows * ncol + HALO * t, rows * ncol + HALO * (t + 2))
        core_msg[at, :] = jnp.where(lower, first, final)
        chip_msg[at, :] = jnp.where(lower, final, first)
    for i, x in enumerate(mats):
        at = slice((rows + HALO) * ncol + half * i, (rows + HALO) * ncol + half * (i + 1))
        core_msg[at, :] = jnp.where(lower, x[:half], x[half:])
        chip_msg[at, :] = jnp.where(lower, x[half:], x[:half])


def shifted(v):
    n = v.shape[1]
    r = v.shape[0]
    return (pltpu.roll(v, n - 1, 1), pltpu.roll(v, 1, 1), pltpu.roll(v, r - 1, 0), pltpu.roll(v, 1, 0))


def scaled_apply(v, east, west, south, north):
    e, w, s, n = shifted(v)
    return v - east * e - west * w - south * s - north * n


def middle(b, r, c, l, w, mflat, got, s2, s1, pre_o, z_o, east_o, west_o, south_o, north_o, wt, mwin, msg):
    late_windows(w, mflat, got, s1, s2, wt, mwin)
    upper = lax.axis_index("core") == 0
    left, right = side_block(got, -1), side_block(got, 1)
    rows = 4 * HALO
    tiles = range(b.shape[1] // LANES + 2)
    pair, chip = [jnp.concatenate([x[rows * t : rows * (t + 1), :] for t in tiles], axis=1) for x in (s1, s2)]
    above, below = jnp.where(upper, chip, pair), jnp.where(upper, pair, chip)
    wins = []
    for i, x in enumerate((b, l, r, c)):
        at = slice(HALO * i, HALO * (i + 1))
        wins.append(jnp.concatenate([halves(left, x, right, i), below[at], above[at]], axis=0))
    bw, lw, rw, cw = wins
    n = bw.shape[1]
    ncol = n // LANES - 2
    row = lax.broadcasted_iota(jnp.int32, bw.shape, 0)
    far = jnp.logical_or(row == 11, row == 12)
    inside = jnp.logical_and(lw > 0.0, jnp.logical_not(far))
    diag, inv, coef = operator(lw, rw, cw, inside)
    z = jnp.where(far, bw, bw * inv)
    d = z * (1.0 / THETA)
    x = d
    z = jnp.where(far, lw, z - scaled_apply(d, *coef))
    d = (RHO1 * RHO0) * d + (2.0 * RHO1 / DELTA) * z
    x = x + d
    z = z - scaled_apply(d, *coef)
    d = (RHO2 * RHO1) * d + (2.0 * RHO2 / DELTA) * z
    x = x + d
    z = z - scaled_apply(d, *coef)
    own = slice(0, 8)
    g = diag[own] * (z - OMEGA * scaled_apply(z, *coef))[own]
    part = jnp.zeros((8, LANES), jnp.float32)
    for t in range(ncol):
        part = part + w[:, t * LANES : (t + 1) * LANES] * g[:, (t + 1) * LANES : (t + 2) * LANES]
    pre_o[...] = x
    z_o[...] = z
    for ref, value in zip((east_o, west_o, south_o, north_o), coef):
        ref[...] = value
    total = jnp.sum(part, axis=1, keepdims=True)
    place = lax.axis_index("z") * 4
    lane = lax.broadcasted_iota(jnp.int32, (8, LANES), 1)
    row = lax.broadcasted_iota(jnp.int32, (8, LANES), 0)
    spread = jnp.where(lane == place + row // 2, total, 0.0)
    msg[...] = jnp.broadcast_to(jnp.sum(spread, axis=0, keepdims=True)[None], msg.shape)


def reordered(m):
    n = m.shape[0]
    i = lax.broadcasted_iota(jnp.int32, (LANES, LANES), 0)
    o = lax.broadcasted_iota(jnp.int32, (LANES, LANES), 1)
    source = (o % 64) // 4 * 8 + o % 4

    def pick(rows, core, high):
        chosen = jnp.logical_and(o // 64 == high, i == source + 4 * core)
        return jnp.dot(
            rows, chosen.astype(jnp.float32), precision=lax.Precision.HIGHEST, preferred_element_type=jnp.float32
        )

    even = pick(m, 0, 0) + pick(pltpu.roll(m, n - 1, 0), 0, 1)
    odd = pick(pltpu.roll(m, 1, 0), 1, 0) + pick(m, 1, 1)
    row = lax.broadcasted_iota(jnp.int32, m.shape, 0)
    return jnp.where(row % 2 == 0, even, odd)


def late_windows(w, mflat, got, s1, s2, wt, mwin):
    upper = lax.axis_index("core") == 0
    left, right = side_block(got, -1), side_block(got, 1)
    ww = halves(left, w, right, 4)
    ncol = ww.shape[1] // LANES
    pair, chip = s1[4 * HALO * ncol :, :], s2[4 * HALO * ncol :, :]
    above, below = jnp.where(upper, chip, pair), jnp.where(upper, pair, chip)
    for t in range(ncol):
        at = slice(HALO * t, HALO * (t + 1))
        s = slice(t * LANES, (t + 1) * LANES)
        wt[:, s] = jnp.concatenate([ww[:, s], below[at], above[at]], axis=0)
    half = mflat.shape[0] // 2
    parts = []
    for i, mine in enumerate((left[40:], mflat[...], right[40:])):
        at = slice(HALO * ncol + half * i, HALO * ncol + half * (i + 1))
        parts += [above[at], mine, below[at]]
    mwin[...] = jnp.concatenate(parts, axis=0)


def last(xs, gathered, mwin, pre, z_i, wt, east, west, south, north, out):
    ncols = lax.axis_size("cols")
    tiles = mwin.shape[0] // 24
    mats = [[mwin[tiles * (8 * g + k) : tiles * (8 * g + k + 1), :] for k in range(8)] for g in range(3)]
    me = lax.axis_index("cols")

    def corrections(group, mats):
        v = jnp.concatenate([gathered[at * ncols + group] for at in range(2 * xs)], axis=0)
        lines = []
        for m in mats[2:] + mats[:2]:
            p = jnp.sum(m * v, axis=0, keepdims=True)
            lines += [p, p]
        return jnp.sum(jnp.concatenate(lines, axis=0), axis=1, keepdims=True)

    cl = corrections(jnp.maximum(me - 1, 0), mats[0])
    co = corrections(me, mats[1])
    cn = corrections(jnp.minimum(me + 1, ncols - 1), mats[2])
    w = wt[...]
    n = w.shape[1]
    lane = lax.broadcasted_iota(jnp.int32, (1, n), 1)
    lifted = w * jnp.where(lane < LANES, cl, jnp.where(lane >= n - LANES, cn, co))
    op = functools.partial(scaled_apply, east=east[...], west=west[...], south=south[...], north=north[...])
    e = lifted - OMEGA * op(lifted)
    x = pre[...] + e
    z = z_i[...] - op(e)
    d = z * (1.0 / THETA)
    x = x + d
    z = z - op(d)
    d = (RHO1 * RHO0) * d + (2.0 * RHO1 / DELTA) * z
    x = x + d
    z = z - op(d)
    d = (RHO2 * RHO1) * d + (2.0 * RHO2 / DELTA) * z
    x = x + d
    out[...] = x[0:8, LANES : n - LANES]


def local(sizes, rhs, cond_row, cond_col, leak, agg_members, coarse_inverse):
    xs, zs, cores, cols = sizes
    width = rhs.shape[1]
    wide = width + 2 * LANES
    m = coarse_inverse[0]
    tiles = m.shape[1] // LANES
    group = agg_members.shape[2] // 4
    agg = agg_members[0, 0]
    block = f32(8, width)
    edges = call(
        functools.partial(first_kernel, group),
        f32(cols, 8 + 4 * tiles, LANES),
        6,
        "first",
        space=pltpu.HBM,
        limit=FIRST_LIMIT,
        scratch=[pltpu.VMEM((8, width), jnp.float32)] * 4
        + [
            pltpu.VMEM(agg.shape, jnp.int32),
            pltpu.VMEM(m.shape, jnp.float32),
            pltpu.VMEM((8, width), jnp.float32),
            pltpu.VMEM((4 * tiles, LANES), jnp.float32),
            pltpu.SemaphoreType.DMA((10,)),
        ],
    )(rhs, cond_row, cond_col, leak, agg, m)
    b, r, c, l = rhs, cond_row, cond_col, leak
    got = lax.all_to_all(edges, "cols", 0, 0, tiled=True)
    devices = xs * zs * cores
    swap = []
    for i in range(1, devices - 1, 2):
        swap += [(i, i + 1), (i + 1, i)]
    message = f32((4 * HALO + HALO) * wide // LANES + 6 * tiles, LANES)
    chip_msg, core_msg, w, mflat = call(
        functools.partial(rows_kernel, group), [message, message, block, f32(4 * tiles, LANES)], 6, "rows"
    )(b, r, c, l, agg, got)
    s2 = lax.ppermute(chip_msg, ROWAX, swap)
    s1 = lax.ppermute(core_msg, "core", [(0, 1), (1, 0)])
    win = f32(WROWS, wide)
    pre, z, east, west, south, north, wt, mwin, msg = call(
        middle, [win] * 7 + [f32(24 * tiles, LANES), f32(zs, 1, LANES)], 9, "middle"
    )(b, r, c, l, w, mflat, got, s2, s1)
    spread = lax.all_to_all(msg, "z", 0, 0, tiled=True)
    line = jnp.sum(spread, axis=0)
    second = jnp.broadcast_to(line[None], (xs * cores * cols, 1, LANES))
    gathered = lax.all_to_all(second, ("x", "core", "cols"), 0, 0, tiled=True)
    return call(functools.partial(last, xs), block, 9, "last")(
        gathered, mwin, pre, z, wt, east, west, south, north
    )


def solution(mesh):
    rows, cols = mesh.shape["rows"], mesh.shape["cols"]
    cores = 2
    xs = 4 if rows == 256 else 2
    zs = rows // (xs * cores)
    fine = Mesh(mesh.devices.reshape(xs, zs, cores, cols), ("x", "z", "core", "cols"))
    spec = P(ROWAX, "cols")
    in_specs = (spec, spec, spec, spec, P(ROWAX, "cols", None, None), P("cols", ROWAX, None))
    return jax.shard_map(
        functools.partial(local, (xs, zs, cores, cols)),
        mesh=fine,
        in_specs=in_specs,
        out_specs=spec,
        check_vma=False,
    )
```
